128 devices in a mesh: dp: 8 (over x, y_lo), tensor: 16 (over y_hi, z, core).
Axes of the slice: x: 4, y: 4 (y_hi: 2, y_lo: 2; y = y_hi * 2 + y_lo), z: 4, core: 2. Of those that a mesh axis runs over, the one named last changes fastest.
Arguments:
- hidden_in: bfloat16 [2048, 8192], P('dp', 'tensor'), may hold values from -6 to 6
- norm_gain: float32 [8192], replicated, may hold values from 0.5 to 1.5
- clip_base: float32 [8192], replicated, may hold values from 0.5 to 2
- pct_index: int32 [8192], replicated, may hold values from 0 to 63
- clip_step: float32 [8192], replicated, may hold values from -4 to 4
- w_query: bfloat16 [8192, 8192], P(None, 'tensor'), may hold values from -1 to 1
- w_key: bfloat16 [8192, 1024], P(None, 'tensor'), may hold values from -1 to 1
- w_value: bfloat16 [8192, 1024], P(None, 'tensor'), may hold values from -0.0625 to 0.0625
- w_out: bfloat16 [8192, 8192], P('tensor'), may hold values from -0.0625 to 0.0625
- doc_ids: int32 [8, 256], P('dp'), may hold values from 0 to 3, never falling along the last dimension, each value on 1 to 128 neighbouring positions
Outputs:
- tangent_out: bfloat16 [2048, 8192], P('dp', 'tensor')
- gn_product: float32 [8192], P('tensor')
The draws below stay inside these ranges and needn't reach their ends.
Inputs may be any that keep to these rules, and one draw needn't show every extreme that they name: `doc_ids`: document numbers never fall along a sequence; each document holds 1 to 128 positions.
All inputs are finite; a program needn't handle non-finite values.
Results may differ from the reference program's by a relative error of at most 0.02.
The reference program's roundings to bfloat16 on the way count: a program that leaves them out, or rounds other values in their place, can miss the bound.
Values may be sent and summed in bfloat16 or wider, within the bound.
A program may use at most 128 MiB of HBM per device.

```python
import math
import jax
import jax.numpy as jnp
import numpy as np
from jax import lax

D = 8192
HEADS = 64
KV_HEADS = 8
HEAD_DIM = 128
SEQ = 256
TOKENS = 2048
N_DP = 8
N_TENSOR = 16


def draw_w_query(key, part):
    base = jnp.clip(jax.random.normal(jax.random.fold_in(key, 7), (D, HEADS, HEAD_DIM), jnp.float32), -4.0, 4.0) / math.sqrt(D)
    return base.reshape(D, HEADS * HEAD_DIM).astype(jnp.bfloat16)


def draw_w_key(key, part):
    base = jnp.clip(jax.random.normal(jax.random.fold_in(key, 13), (D, KV_HEADS, HEAD_DIM), jnp.float32), -4.0, 4.0) / math.sqrt(D)
    return jnp.transpose(base, (0, 2, 1)).reshape(D, KV_HEADS * HEAD_DIM).astype(jnp.bfloat16)


def plant(drawn, own_key, smallest, largest):
    index_at = [jax.random.randint(jax.random.fold_in(own_key, axis), (), 0, length) for axis, length in enumerate(drawn.shape)]
    main_axis = drawn.shape.index(max(drawn.shape))
    next_to = index_at[:main_axis] + [(index_at[main_axis] + 1) % drawn.shape[main_axis]] + index_at[main_axis + 1:]
    return drawn.at[tuple(index_at)].set(smallest).at[tuple(next_to)].set(largest)


def shard_levels(rng, extent, split, smallest, top_value):
    def one(axis_at, blocks):
        steps = jax.random.uniform(jax.random.fold_in(jax.random.fold_in(rng, 6), axis_at), (blocks,), jnp.float32, smallest / len(split), top_value / len(split))
        return jnp.repeat(jnp.exp(steps), extent[axis_at] // blocks).reshape((-1,) + (1,) * (len(extent) - axis_at - 1))

    gain = one(*split[0])
    for cut in split[1:]:
        gain = gain * one(*cut)
    return gain


def profile(number_of, total, most, skew):
    portions = [(1 << 20) // math.isqrt(rank ** skew) + 1 for rank in range(2, number_of + 1)]
    spare, counts = total - most - (number_of - 1), [1] * (number_of - 1)
    while spare > 0:
        movable = [i for i in range(number_of - 1) if counts[i] < most]
        mass, remaining = sum([portions[i] for i in movable]), spare
        for i in movable:
            more = min(most - counts[i], max(1, remaining * portions[i] // mass), spare)
            counts[i] = counts[i] + more
            spare = spare - more
    return np.array([most] + counts)


def uneven_parts(stream_key, count, total, limit, skew):
    if count == 2:
        one = jax.random.randint(stream_key, (), max(1, total - limit), min(limit, total - 1) + 1)
        return jnp.stack([one, total - one])
    tallies = jnp.asarray(profile(count, total, limit, skew), jnp.int32)
    twos = (count - 1) // 2
    donor, receiver = tallies[1:1 + 2 * twos:2], tallies[2:2 + 2 * twos:2]
    room = jnp.minimum(donor - 1, limit - receiver)
    shifted = jax.random.randint(jax.random.fold_in(stream_key, 1), (twos,), 0, 1 << 20) % (room + 1)
    tallies = tallies.at[1:1 + 2 * twos:2].set(donor - shifted).at[2:2 + 2 * twos:2].set(receiver + shifted)
    return tallies[jax.random.permutation(jax.random.fold_in(stream_key, 2), count)]


def centred(key, extent, scale, reach, shards=(), kind=jnp.bfloat16):
    level = shard_levels(key, extent, shards, -0.22, 0.18) if shards else 1.0
    drawn = jax.random.normal(key, extent, jnp.float32) * scale * level
    return jnp.minimum(jnp.maximum(drawn, -reach), reach).astype(kind)


def setup_inputs(seed: int = 0) -> dict:
    key_list = jax.random.split(jax.random.key(seed), 11)
    return {
        "hidden_in": centred(key_list[0], (TOKENS, D), 1.0, 6.0, ((0, 8), (1, 16))),
        "norm_gain": jnp.clip(1.0 + 0.1 * jax.random.normal(key_list[1], (D,), jnp.float32), 0.5, 1.5),
        "clip_base": jnp.clip(jnp.exp(jax.random.uniform(key_list[2], (D,), jnp.float32, math.log(0.5), math.log(2.0))), 0.5, 2.0),
        "pct_index": plant(jax.random.randint(key_list[3], (D,), 0, 64), jax.random.fold_in(key_list[3], 1), 0, 63).astype(jnp.int32),
        "clip_step": centred(key_list[4], (D,), 1.0, 4.0, (), jnp.float32),
        "w_query": draw_w_query(jax.random.fold_in(key_list[10], 71), 0),
        "w_key": draw_w_key(jax.random.fold_in(key_list[10], 71), 0),
        "w_value": centred(key_list[7], (D, KV_HEADS * HEAD_DIM), D ** -0.5, 0.0625, ((1, 16),)),
        "w_out": centred(key_list[8], (HEADS * HEAD_DIM, D), (HEADS * HEAD_DIM) ** -0.5, 0.0625, ((0, 16),)),
        "doc_ids": jax.vmap(lambda own: jnp.searchsorted(jnp.cumsum(uneven_parts(own, 4, SEQ, SEQ // 2, 0)), jnp.arange(SEQ), side="right"))(jax.random.split(key_list[9], N_DP)).reshape((N_DP, SEQ)).astype(jnp.int32),
    }


EPSILON = 1e-05
ROPE_BASE = 500000.0
MASKED = -1e+30

def rope_tables(token_count, head_size):
    positions = jnp.arange(token_count, dtype=jnp.float32)
    frequency = jnp.exp(-math.log(ROPE_BASE) * 2.0 * jnp.arange(head_size // 2, dtype=jnp.float32) / head_size)
    angles = positions[:, None] * frequency[None, :]
    return (jnp.cos(angles)[:, None, :], jnp.sin(angles)[:, None, :])

def rotate(values, cosine, sine_part, turning):
    half_dim = values.shape[-1] // 2
    front_part = values[..., :half_dim]
    back_part = values[..., half_dim:]
    return jnp.concatenate([front_part * cosine - turning * back_part * sine_part, back_part * cosine + turning * front_part * sine_part], axis=-1)

def clip_parts(token_rows, norm_gain, thresh, clip_step, width):
    rows_float = token_rows.astype(jnp.float32)
    mean_square = lax.optimization_barrier(jnp.sum(rows_float * rows_float, axis=-1, keepdims=True)) / width
    normed = rows_float * lax.rsqrt(mean_square + EPSILON) * norm_gain
    ratios = normed / thresh
    bent_vals = jnp.tanh(ratios)
    clipped = (thresh * bent_vals).astype(jnp.bfloat16)
    slopes = bent_vals - ratios * (1.0 - bent_vals * bent_vals)
    tangent = (slopes * clip_step).astype(jnp.bfloat16)
    return (clipped, tangent, slopes)

def reference(hidden_in, norm_gain, clip_base, pct_index, clip_step, w_query, w_key, w_value, w_out, doc_ids):
    thresh = clip_base * (1.0 + pct_index.astype(jnp.float32) / 32.0)
    sequences = hidden_in.reshape(N_DP, SEQ, D)
    cosine, sine_part = rope_tables(SEQ, HEAD_DIM)
    score_scale = HEAD_DIM ** (-0.5)
    head_group = HEADS // KV_HEADS
    f32 = jnp.float32
    bf16 = jnp.bfloat16

    def head_major(raw_vals):
        return jnp.transpose(raw_vals.reshape(SEQ, HEAD_DIM, KV_HEADS), (0, 2, 1))

    def one_sequence(inputs):
        token_rows, doc_row = inputs
        clipped, tangent, slopes = clip_parts(token_rows, norm_gain, thresh, clip_step, D)

        def project_query(source):
            raw_vals = jnp.dot(source, w_query, preferred_element_type=f32).reshape(SEQ, HEADS, HEAD_DIM)
            return rotate(raw_vals, cosine, sine_part, 1.0).astype(bf16)

        def project_key(source):
            raw_vals = jnp.dot(source, w_key, preferred_element_type=f32).astype(bf16)
            shaped = head_major(raw_vals.astype(f32))
            return jnp.repeat(rotate(shaped, cosine, sine_part, 1.0).astype(bf16), head_group, axis=1)

        def project_value(source):
            raw_vals = jnp.dot(source, w_value, preferred_element_type=f32).astype(bf16)
            return jnp.repeat(head_major(raw_vals), head_group, axis=1)
        query_p = project_query(clipped).astype(f32)
        query_t = project_query(tangent).astype(f32)
        key_p = project_key(clipped).astype(f32)
        key_t = project_key(tangent).astype(f32)
        value_p = project_value(clipped).astype(f32)
        value_t = project_value(tangent).astype(f32)
        places = jnp.arange(SEQ)
        allowed = (doc_row[:, None] == doc_row[None, :]) & (places[:, None] >= places[None, :])
        scores = jnp.einsum('shd,thd->hst', query_p, key_p) * score_scale
        attn_probs = jax.nn.softmax(jnp.where(allowed[None], scores, MASKED), axis=-1)
        probs_b = attn_probs.astype(bf16).astype(f32)
        tan_scores = (jnp.einsum('shd,thd->hst', query_t, key_p) + jnp.einsum('shd,thd->hst', query_p, key_t)) * score_scale
        tan_probs = (attn_probs * (tan_scores - lax.optimization_barrier(jnp.sum(attn_probs * tan_scores, axis=-1, keepdims=True)))).astype(bf16).astype(f32)
        tan_ctx = (jnp.einsum('hst,thd->shd', tan_probs, value_p) + jnp.einsum('hst,thd->shd', probs_b, value_t)).astype(bf16)
        tan_ctx = tan_ctx.reshape(SEQ, N_TENSOR, HEADS * HEAD_DIM // N_TENSOR).astype(f32)
        group_parts = jnp.einsum('sgc,gcd->gsd', tan_ctx, w_out.reshape(N_TENSOR, HEADS * HEAD_DIM // N_TENSOR, D).astype(f32))
        rounded = lax.optimization_barrier(group_parts.astype(bf16)).astype(f32)
        tangent_rows = lax.optimization_barrier(jnp.sum(rounded, axis=0)).astype(bf16)
        back_ctx = jnp.dot(tangent_rows, w_out.T, preferred_element_type=f32).astype(bf16)
        back_ctx = back_ctx.reshape(SEQ, HEADS, HEAD_DIM).astype(f32)
        grad_prob = jnp.einsum('shd,thd->hst', back_ctx, value_p)
        grad_score = (attn_probs * (grad_prob - lax.optimization_barrier(jnp.sum(attn_probs * grad_prob, axis=-1, keepdims=True))) * score_scale).astype(bf16).astype(f32)
        grad_query = rotate(jnp.einsum('hst,thd->shd', grad_score, key_p), cosine, sine_part, -1.0).astype(bf16)
        grad_query = grad_query.reshape(SEQ, HEADS * HEAD_DIM)
        key_heads = rotate(jnp.einsum('hst,shd->thd', grad_score, query_p), cosine, sine_part, -1.0)
        value_heads = jnp.einsum('hst,shd->thd', probs_b, back_ctx)

        def head_total(per_head):
            per_device = lax.optimization_barrier(jnp.sum(per_head.reshape(SEQ, N_TENSOR, HEADS // N_TENSOR, HEAD_DIM), axis=2))
            dev_rounded = lax.optimization_barrier(per_device.astype(bf16)).astype(f32)
            summed = lax.optimization_barrier(jnp.sum(dev_rounded.reshape(SEQ, KV_HEADS, N_TENSOR // KV_HEADS, HEAD_DIM), axis=2))
            return jnp.transpose(summed, (0, 2, 1)).astype(bf16).reshape(SEQ, KV_HEADS * HEAD_DIM)
        grad_key = head_total(key_heads)
        grad_value = head_total(value_heads)
        grad_in = jnp.dot(grad_query, w_query.T, preferred_element_type=f32) + jnp.dot(grad_key, w_key.T, preferred_element_type=f32) + jnp.dot(grad_value, w_value.T, preferred_element_type=f32)
        channel = lax.optimization_barrier(jnp.sum(grad_in * slopes, axis=0))
        return (tangent_rows, channel)
    outputs = lax.map(one_sequence, (sequences, doc_ids))
    return (outputs[0].reshape(TOKENS, D), lax.optimization_barrier(jnp.sum(outputs[1], axis=0)) / TOKENS)
```

```python
import functools
import math

import jax
import jax.numpy as jnp
from jax import lax
from jax.experimental import pallas as pl
from jax.experimental.pallas import tpu as pltpu
from jax.sharding import PartitionSpec as P

HEAD_DIM = 128
EPSILON = 1e-05
ROPE_BASE = 500000.0
MASKED = -1e30
MESH = pl.DeviceIdType.MESH
f32 = jnp.float32
bf16 = jnp.bfloat16

N_Y, N_Z, N_C = 2, 4, 2
N_T = N_Y * N_Z * N_C
TOK = 256
SHARD = 512
WIDTH = N_T * SHARD

RELS = [(dy, dz, dc) for dy in range(N_Y) for dz in range(N_Z) for dc in range(N_C)]
PEERS = [r for r in RELS if r != (0, 0, 0)]
CHIPS = [(0, 0), (0, 1), (0, 3), (1, 0), (0, 2), (1, 1), (1, 3), (1, 2)]


def ridx(rel):
    return (rel[0] * N_Z + rel[1]) * N_C + rel[2]


def peer(me, rel):
    y, z, c = me // (N_Z * N_C), (me // N_C) % N_Z, me % N_C
    y = (y + rel[0]) % N_Y
    z = (z + rel[1]) % N_Z
    c = (c + rel[2]) % N_C
    return (y * N_Z + z) * N_C + c


def source(me, rel):
    return peer(me, (-rel[0], -rel[1], -rel[2]))


def remote(src, dst, ssem, rsem, dp, target):
    return pltpu.make_async_remote_copy(
        src_ref=src, dst_ref=dst, send_sem=ssem, recv_sem=rsem, device_id=(dp, target), device_id_type=MESH
    )


def nt(a, b):
    return lax.dot_general(a, b, (((1,), (1,)), ((), ())), preferred_element_type=f32)


def tn(a, b):
    return lax.dot_general(a, b, (((0,), (0,)), ((), ())), preferred_element_type=f32)


def permutation():
    row = lax.broadcasted_iota(jnp.int32, (128, 128), 0)
    col = lax.broadcasted_iota(jnp.int32, (128, 128), 1)
    head, low = row // 16, row % 16
    want = jnp.where(low < 8, low * 8 + head, 64 + (low - 8) * 8 + head)
    return (col == want).astype(f32).astype(bf16)


def k1_body(
    x_ref, gain_ref, base_ref, pct_ref, step_ref, wq_hbm, wk_hbm, wv_hbm, cos_ref, sin_ref, cost_ref, sint_ref,
    qp_out, qt_out, kp_out, kt_out, vp_out, vt_out, rs_out, hid_out,
    hid, xs, wq, wkv, ss_send, ssr, rs, kvacc, qacc, kvt, kvr,
    wsem, hs, hr, fs, sss, ssrs, kvs, kvrs,
):
    me = lax.axis_index("tensor")
    dp = lax.axis_index("dp")
    barrier = pltpu.get_barrier_semaphore()
    for rel in PEERS:
        pl.semaphore_signal(barrier, inc=1, device_id=(dp, peer(me, rel)), device_id_type=MESH)
    loads = [
        pltpu.make_async_copy(wk_hbm, wkv.at[pl.ds(0, 64)], wsem.at[0]),
        pltpu.make_async_copy(wv_hbm, wkv.at[pl.ds(64, 64)], wsem.at[1]),
        pltpu.make_async_copy(wq_hbm, wq, wsem.at[2]),
    ]
    for load in loads:
        load.start()

    own = x_ref[...].astype(f32)
    square = own * own
    high = square.astype(bf16)
    low = (square - high.astype(f32)).astype(bf16)
    ones = jnp.ones((8, SHARD), bf16)
    ss_send[...] = nt(ones, high) + nt(ones, low)
    ssr[me] = ss_send[...]
    hid[me] = x_ref[...]

    pl.semaphore_wait(barrier, len(PEERS))
    sends = []
    for rel in PEERS:
        i = ridx(rel)
        cp = remote(ss_send, ssr.at[me], sss.at[i], ssrs.at[i], dp, peer(me, rel))
        cp.start()
        sends.append(cp)
    cp = remote(x_ref, hid.at[me], hs.at[1], hr.at[1], dp, peer(me, (0, 0, 1)))
    cp.start()
    sends.append(cp)
    for dy, dz in CHIPS[1:]:
        i = ridx((dy, dz, 0))
        cp = remote(x_ref, hid.at[me], hs.at[i], hr.at[i], dp, peer(me, (dy, dz, 0)))
        cp.start()
        sends.append(cp)
    for rel in PEERS:
        i = ridx(rel)
        remote(ss_send, ssr.at[source(me, rel)], sss.at[i], ssrs.at[i], dp, peer(me, rel)).wait_recv()
    total = jnp.sum(ssr[...], axis=0)
    scale = lax.rsqrt(total / WIDTH + EPSILON)
    rs[...] = jnp.transpose(jnp.broadcast_to(scale[0:1, :], (128, TOK)))
    rs_out[...] = rs[...]

    kvacc[...] = jnp.zeros_like(kvacc)

    def work(j):
        lanes = pl.ds(pl.multiple_of(j * SHARD, SHARD), SHARD)
        thresh = base_ref[:, lanes] * (1.0 + pct_ref[:, lanes].astype(f32) / 32.0)
        over = gain_ref[:, lanes] / thresh
        step = step_ref[:, lanes]

        def rows_step(r, carry):
            rows = pl.ds(pl.multiple_of(r * 32, 32), 32)
            rest = pl.ds(pl.multiple_of(TOK + r * 32, 32), 32)
            x = hid[j, rows, :].astype(f32)
            scale = rs[rows, :]
            for l in range(SHARD // 128):
                cut = slice(l * 128, l * 128 + 128)
                ratio = x[:, cut] * scale * over[:, cut]
                bent = jnp.tanh(ratio)
                xs[j, rows, cut] = (thresh[:, cut] * bent).astype(bf16)
                slope = bent - ratio * (1.0 - bent * bent)
                xs[j, rest, cut] = (slope * step[:, cut]).astype(bf16)
            return carry

        lax.fori_loop(0, TOK // 32, rows_step, 0)
        kvacc[...] += nt(xs[j], wkv[:, lanes])

    loads[0].wait()
    loads[1].wait()
    for dy, dz in CHIPS:
        if (dy, dz) != (0, 0):
            i = ridx((dy, dz, 0))
            j = source(me, (dy, dz, 0))
            remote(x_ref, hid.at[j], hs.at[i], hr.at[i], dp, me).wait_recv()
            i1 = ridx((dy, dz, 1))
            cp = remote(hid.at[j], hid.at[j], fs.at[i1], hr.at[i1], dp, peer(me, (0, 0, 1)))
            cp.start()
            sends.append(cp)
        work(source(me, (dy, dz, 0)))
        i1 = ridx((dy, dz, 1))
        j1 = source(me, (dy, dz, 1))
        remote(x_ref, hid.at[j1], hs.at[i1], hr.at[i1], dp, me).wait_recv()
        work(j1)

    kvt[...] = nt(permutation(), kvacc[...].astype(bf16)).astype(bf16)

    def block(chip):
        return pl.ds(pl.multiple_of(chip * 16, 16), 16)

    kvr[me] = kvt[block(me // N_C), :]
    for rel in PEERS:
        i = ridx(rel)
        to = peer(me, rel)
        cp = remote(kvt.at[block(to // N_C)], kvr.at[me], kvs.at[i], kvrs.at[i], dp, to)
        cp.start()
        sends.append(cp)

    loads[2].wait()
    qacc[...] = jnp.zeros_like(qacc)

    def q_step(j, carry):
        rows = pl.ds(pl.multiple_of(j * SHARD, SHARD), SHARD)
        qacc[...] += jnp.dot(xs[j], wq[rows, :], preferred_element_type=f32)
        return carry

    lax.fori_loop(0, N_T, q_step, 0)
    for h in range(4):
        cut = slice(h * 128, h * 128 + 128)
        for out, top in ((qp_out, 0), (qt_out, TOK)):
            z = qacc[pl.ds(top, TOK), cut]
            out[:, cut] = (z * cos_ref[...] + pltpu.roll(z, 64, 1) * sin_ref[...]).astype(bf16)

    for rel in PEERS:
        i = ridx(rel)
        remote(kvt.at[pl.ds(0, 16)], kvr.at[source(me, rel)], kvs.at[i], kvrs.at[i], dp, me).wait_recv()
    both = kvr[...].astype(f32)
    keys = both[:, 0:8, :].reshape(HEAD_DIM, 2 * TOK)
    vals = both[:, 8:16, :].reshape(HEAD_DIM, 2 * TOK).astype(bf16)
    vp_out[...] = vals[:, :TOK]
    vt_out[...] = vals[:, TOK:]
    cost, sint = cost_ref[...], sint_ref[...]
    for out, left in ((kp_out, 0), (kt_out, TOK)):
        z = keys[:, left : left + TOK]
        front, back = z[:64], z[64:]
        out[0:64, :] = (front * cost - back * sint).astype(bf16)
        out[64:128, :] = (back * cost + front * sint).astype(bf16)
    cp = pltpu.make_async_copy(hid, hid_out, wsem.at[0])
    cp.start()
    cp.wait()
    for cp in sends:
        cp.wait_send()


VM = pl.BlockSpec(memory_space=pltpu.VMEM)
ANY = pl.BlockSpec(memory_space=pl.ANY)


def k1(x, gain, base, pct, step, wq, wkt, wvt, cos, sin, cost, sint):
    sds = jax.ShapeDtypeStruct
    dma = pltpu.SemaphoreType.DMA((N_T,))
    return pl.pallas_call(
        k1_body,
        name="project",
        out_shape=[sds((TOK, SHARD), bf16)] * 2
        + [sds((HEAD_DIM, TOK), bf16)] * 4
        + [sds((TOK, 128), f32), sds((N_T, TOK, SHARD), bf16)],
        in_specs=[VM] * 5 + [ANY] * 3 + [VM] * 4,
        out_specs=[VM] * 7 + [ANY],
        scratch_shapes=[
            pltpu.VMEM((N_T, TOK, SHARD), bf16),
            pltpu.VMEM((N_T, 2 * TOK, SHARD), bf16),
            pltpu.VMEM((WIDTH, SHARD), bf16),
            pltpu.VMEM((128, WIDTH), bf16),
            pltpu.VMEM((8, TOK), f32),
            pltpu.VMEM((N_T, 8, TOK), f32),
            pltpu.VMEM((TOK, 128), f32),
            pltpu.VMEM((2 * TOK, 128), f32),
            pltpu.VMEM((2 * TOK, SHARD), f32),
            pltpu.VMEM((128, 2 * TOK), bf16),
            pltpu.VMEM((N_T, 16, 2 * TOK), bf16),
            pltpu.SemaphoreType.DMA((4,)),
            dma, dma, dma, dma, dma, dma, dma,
        ],
        compiler_params=pltpu.CompilerParams(collective_id=1, has_side_effects=True, vmem_limit_bytes=56 << 20),
    )(x, gain, base, pct, step, wq, wkt, wvt, cos, sin, cost, sint)


def contract_last(left_side, right_side):
    return nt(left_side, right_side)


def rotate(values, cosine, sine_part, turning):
    half_dim = values.shape[-1] // 2
    front_part = values[..., :half_dim]
    back_part = values[..., half_dim:]
    return jnp.concatenate(
        [
            front_part * cosine - turning * back_part * sine_part,
            back_part * cosine + turning * front_part * sine_part,
        ],
        axis=-1,
    )


def on_device(
    hidden_in, norm_gain, clip_base, pct_index, clip_step, w_query, w_key, w_value, w_out, doc_ids
):
    token_count = TOK
    me = lax.axis_index("tensor")
    score_scale = HEAD_DIM ** (-0.5)
    positions = jnp.arange(TOK, dtype=f32)
    frequency = jnp.exp(-math.log(ROPE_BASE) * 2.0 * jnp.arange(64, dtype=f32) / HEAD_DIM)
    angles = positions[:, None] * frequency[None, :]
    cosine, sine = jnp.cos(angles), jnp.sin(angles)
    cos2 = jnp.concatenate([cosine, cosine], axis=1)
    sin2 = jnp.concatenate([-sine, sine], axis=1)
    row = lambda v: v.reshape(1, WIDTH)
    query_p, query_t, kp, kt, vp, vt, rs, hid = k1(
        hidden_in, row(norm_gain), row(clip_base), row(pct_index), row(clip_step),
        w_query, w_key.T, w_value.T, cos2, sin2, cosine.T, sine.T,
    )
    query_p = query_p.reshape(TOK, 4, HEAD_DIM)
    query_t = query_t.reshape(TOK, 4, HEAD_DIM)
    key_p, key_t, value_p, value_t = kp.T, kt.T, vp.T, vt.T
    cosine, sine_part = cosine[:, None, :], sine[:, None, :]
    local_heads = 4
    doc_row = doc_ids[0]
    places = jnp.arange(token_count)
    allowed = (doc_row[:, None] == doc_row[None, :]) & (places[:, None] >= places[None, :])
    scores = jnp.einsum("shd,td->hst", query_p, key_p, preferred_element_type=f32) * score_scale
    attn_probs = jax.nn.softmax(jnp.where(allowed[None], scores, MASKED), axis=-1)
    probs_b = attn_probs.astype(bf16)
    tan_scores = (
        jnp.einsum("shd,td->hst", query_t, key_p, preferred_element_type=f32)
        + jnp.einsum("shd,td->hst", query_p, key_t, preferred_element_type=f32)
    ) * score_scale
    tan_probs = (
        attn_probs * (tan_scores - jnp.sum(attn_probs * tan_scores, axis=-1, keepdims=True))
    ).astype(bf16)
    tan_ctx = (
        jnp.einsum("hst,td->shd", tan_probs, value_p, preferred_element_type=f32)
        + jnp.einsum("hst,td->shd", probs_b, value_t, preferred_element_type=f32)
    ).astype(bf16)
    tan_ctx = tan_ctx.reshape(token_count, local_heads * HEAD_DIM)
    partial_out = jnp.dot(tan_ctx, w_out, preferred_element_type=f32)
    tangent_shard = (
        lax.psum_scatter(
            partial_out.astype(jnp.bfloat16), "tensor", scatter_dimension=1, tiled=True
        )
        .astype(jnp.float32)
        .astype(bf16)
    )
    back_ctx = contract_last(lax.all_gather(tangent_shard, "tensor", axis=1, tiled=True), w_out)
    back_ctx = back_ctx.astype(bf16).reshape(token_count, local_heads, HEAD_DIM)
    grad_prob = jnp.einsum("shd,td->hst", back_ctx, value_p, preferred_element_type=f32)
    grad_score = (
        attn_probs
        * (grad_prob - jnp.sum(attn_probs * grad_prob, axis=-1, keepdims=True))
        * score_scale
    ).astype(bf16)
    grad_query = (
        rotate(
            jnp.einsum("hst,td->shd", grad_score, key_p, preferred_element_type=f32),
            cosine,
            sine_part,
            -1.0,
        )
        .astype(bf16)
        .reshape(token_count, local_heads * HEAD_DIM)
    )
    key_local = jnp.sum(
        rotate(
            jnp.einsum("hst,shd->thd", grad_score, query_p, preferred_element_type=f32),
            cosine,
            sine_part,
            -1.0,
        ),
        axis=1,
    )
    value_local = jnp.einsum("hst,shd->td", probs_b, back_ctx, preferred_element_type=f32)
    key_heads, key_width, key_head = 8, 1024, me // 2
    selector = (jnp.arange(key_heads) == key_head).astype(f32)
    key_placed = (key_local.astype(bf16).astype(f32)[:, :, None] * selector).reshape(
        token_count, key_width
    )
    value_placed = (value_local.astype(bf16).astype(f32)[:, :, None] * selector).reshape(
        token_count, key_width
    )
    grad_key, grad_value = (
        lax.psum_scatter(
            key_placed.astype(jnp.bfloat16), "tensor", scatter_dimension=1, tiled=True
        ).astype(jnp.float32),
        lax.psum_scatter(
            value_placed.astype(jnp.bfloat16), "tensor", scatter_dimension=1, tiled=True
        ).astype(jnp.float32),
    )
    partial_in = (
        contract_last(grad_query, w_query)
        + contract_last(grad_key.astype(bf16), w_key)
        + contract_last(grad_value.astype(bf16), w_value)
    )
    thresh = clip_base * (1.0 + pct_index.astype(f32) / 32.0)
    hidden = jnp.transpose(hid, (1, 0, 2)).reshape(TOK, WIDTH).astype(f32)
    ratios = hidden * rs[:, 0:1] * norm_gain / thresh
    bent = jnp.tanh(ratios)
    slopes = bent - ratios * (1.0 - bent * bent)
    token_total = token_count * lax.axis_size("dp")
    channel = jnp.sum(partial_in * slopes, axis=0) / token_total
    channel = lax.psum_scatter(channel, "tensor", scatter_dimension=0, tiled=True)
    gn_product = lax.psum(channel, "dp")
    return (tangent_shard, gn_product)


def solution(mesh):
    in_specs = (
        P("dp", "tensor"),
        P(),
        P(),
        P(),
        P(),
        P(None, "tensor"),
        P(None, "tensor"),
        P(None, "tensor"),
        P("tensor", None),
        P("dp", None),
    )
    out_specs = (P("dp", "tensor"), P("tensor"))
    return jax.shard_map(
        on_device, mesh=mesh, in_specs=in_specs, out_specs=out_specs, check_vma=False
    )
```

```python
import functools
import math

import jax
import jax.numpy as jnp
import numpy as np
from jax import lax
from jax.experimental import pallas as pl
from jax.experimental.pallas import tpu as pltpu
from jax.sharding import PartitionSpec as P

HEAD_DIM = 128
EPSILON = 1e-05
ROPE_BASE = 500000.0
MASKED = -1e30
MESH = pl.DeviceIdType.MESH
f32 = jnp.float32
bf16 = jnp.bfloat16

N_Y, N_Z, N_C = 2, 4, 2
N_T = N_Y * N_Z * N_C
TOK = 256
SHARD = 512
WIDTH = N_T * SHARD
HEADS = 4
N_DP = 8
VMEM_BYTES = 60 << 20

RELS = [(dy, dz, dc) for dy in range(N_Y) for dz in range(N_Z) for dc in range(N_C)]
PEERS = [r for r in RELS if r != (0, 0, 0)]
CHIPS = [(0, 0), (0, 1), (0, 3), (1, 0), (0, 2), (1, 1), (1, 3), (1, 2)]


def ridx(rel):
    return (rel[0] * N_Z + rel[1]) * N_C + rel[2]


def peer(me, rel):
    y, z, c = me // (N_Z * N_C), (me // N_C) % N_Z, me % N_C
    y = (y + rel[0]) % N_Y
    z = (z + rel[1]) % N_Z
    c = (c + rel[2]) % N_C
    return (y * N_Z + z) * N_C + c


def source(me, rel):
    return peer(me, (-rel[0], -rel[1], -rel[2]))


def remote(src, dst, ssem, rsem, dp, target):
    return pltpu.make_async_remote_copy(
        src_ref=src, dst_ref=dst, send_sem=ssem, recv_sem=rsem, device_id=(dp, target), device_id_type=MESH
    )


def nt(a, b):
    return lax.dot_general(a, b, (((1,), (1,)), ((), ())), preferred_element_type=f32)


def tn(a, b):
    return lax.dot_general(a, b, (((0,), (0,)), ((), ())), preferred_element_type=f32)


def permutation():
    row = lax.broadcasted_iota(jnp.int32, (128, 128), 0)
    col = lax.broadcasted_iota(jnp.int32, (128, 128), 1)
    head, low = row // 16, row % 16
    want = jnp.where(low < 8, low * 8 + head, 64 + (low - 8) * 8 + head)
    return (col == want).astype(f32).astype(bf16)


def body(
    x_ref, gain_ref, base_ref, pct_ref, step_ref, doc_ref, cos_ref, sin_ref, cost_ref, sint_ref,
    wq_hbm, wk_hbm, wv_hbm, wo_hbm,
    out_ref, gn_ref,
    hid, xs, slopes, wq, wkv, wo, ss_send, ssr, rs, kvacc, qacc, kvt, kvr, qp, qt, kp, kt, vp, vt, docs, probs, ctx,
    pair_out, pair_in, part_out, part_in, tg, bacc, gq, gkv_out, gkv_in, gkv, gnv, gnv_in, dpv, dpv_in,
    wsem, hs, hr, fs, sss, ssrs, kvs, kvrs, ps, pr, qs, qr, gs, gr, gf, ks, kr, ns, nr, ds, dr,
):
    me = lax.axis_index("tensor")
    dp = lax.axis_index("dp")
    sibling = peer(me, (0, 0, 1))
    barrier = pltpu.get_barrier_semaphore()
    for rel in PEERS:
        pl.semaphore_signal(barrier, inc=1, device_id=(dp, peer(me, rel)), device_id_type=MESH)
    for d in range(1, N_DP):
        pl.semaphore_signal(barrier, inc=1, device_id=((dp + d) % N_DP, me), device_id_type=MESH)
    loads = [
        pltpu.make_async_copy(wk_hbm, wkv.at[pl.ds(0, 64)], wsem.at[0]),
        pltpu.make_async_copy(wv_hbm, wkv.at[pl.ds(64, 64)], wsem.at[1]),
        pltpu.make_async_copy(wq_hbm, wq, wsem.at[2]),
        pltpu.make_async_copy(wo_hbm, wo, wsem.at[3]),
    ]
    for load in loads:
        load.start()

    sends = []

    def send(src, dst, ssem, rsem, to, group=None):
        cp = remote(src, dst, ssem, rsem, dp if group is None else group, to)
        cp.start()
        sends.append(cp)

    def arrived(dst, ssem, rsem):
        remote(dst, dst, ssem, rsem, dp, me).wait_recv()

    own = x_ref[...].astype(f32)
    square = own * own
    high = square.astype(bf16)
    low = (square - high.astype(f32)).astype(bf16)
    ones = jnp.ones((8, SHARD), bf16)
    ss_send[...] = nt(ones, high) + nt(ones, low)
    ssr[me] = ss_send[...]
    hid[me] = x_ref[...]
    docs[...] = jnp.transpose(jnp.broadcast_to(doc_ref[...].astype(f32), (128, TOK)))

    pl.semaphore_wait(barrier, len(PEERS) + N_DP - 1)
    for rel in PEERS:
        i = ridx(rel)
        send(ss_send, ssr.at[me], sss.at[i], ssrs.at[i], peer(me, rel))
    send(x_ref, hid.at[me], hs.at[1], hr.at[1], sibling)
    for dy, dz in CHIPS[1:]:
        i = ridx((dy, dz, 0))
        send(x_ref, hid.at[me], hs.at[i], hr.at[i], peer(me, (dy, dz, 0)))
    for rel in PEERS:
        i = ridx(rel)
        arrived(ssr.at[source(me, rel)], sss.at[i], ssrs.at[i])
    total = jnp.sum(ssr[...], axis=0)
    scale = lax.rsqrt(total / WIDTH + EPSILON)
    rs[...] = jnp.transpose(jnp.broadcast_to(scale[0:1, :], (128, TOK)))

    kvacc[...] = jnp.zeros_like(kvacc)

    def lanes_of(j):
        return pl.ds(pl.multiple_of(j * SHARD, SHARD), SHARD)

    def work(j):
        lanes = lanes_of(j)
        thresh = base_ref[:, lanes] * (1.0 + pct_ref[:, lanes].astype(f32) / 32.0)
        over = gain_ref[:, lanes] / thresh
        step = step_ref[:, lanes]

        def rows_step(r, carry):
            rows = pl.ds(pl.multiple_of(r * 32, 32), 32)
            rest = pl.ds(pl.multiple_of(TOK + r * 32, 32), 32)
            x = hid[j, rows, :].astype(f32)
            scale = rs[rows, :]
            for l in range(SHARD // 128):
                cut = slice(l * 128, l * 128 + 128)
                ratio = x[:, cut] * scale * over[:, cut]
                bent = jnp.tanh(ratio)
                xs[j, rows, cut] = (thresh[:, cut] * bent).astype(bf16)
                slope = bent - ratio * (1.0 - bent * bent)
                slopes[j, rows, cut] = slope
                xs[j, rest, cut] = (slope * step[:, cut]).astype(bf16)
            return carry

        lax.fori_loop(0, TOK // 32, rows_step, 0)
        kvacc[...] += nt(xs[j], wkv[:, lanes])

    loads[0].wait()
    loads[1].wait()

    def gather(buf, ssem, rsem, fsem, use):
        for dy, dz in CHIPS:
            j = source(me, (dy, dz, 0))
            i1 = ridx((dy, dz, 1))
            if (dy, dz) != (0, 0):
                i = ridx((dy, dz, 0))
                arrived(buf.at[j], ssem.at[i], rsem.at[i])
                send(buf.at[j], buf.at[j], fsem.at[i1], rsem.at[i1], sibling)
            use(j)
            j1 = source(me, (dy, dz, 1))
            arrived(buf.at[j1], ssem.at[i1], rsem.at[i1])
            use(j1)

    gather(hid, hs, hr, fs, work)

    kvt[...] = nt(permutation(), kvacc[...].astype(bf16)).astype(bf16)

    def block(chip):
        return pl.ds(pl.multiple_of(chip * 16, 16), 16)

    kvr[me] = kvt[block(me // N_C), :]
    for rel in PEERS:
        i = ridx(rel)
        to = peer(me, rel)
        send(kvt.at[block(to // N_C)], kvr.at[me], kvs.at[i], kvrs.at[i], to)

    loads[2].wait()
    qacc[...] = jnp.zeros_like(qacc)

    def q_step(j, carry):
        qacc[...] += jnp.dot(xs[j], wq[lanes_of(j), :], preferred_element_type=f32)
        return carry

    lax.fori_loop(0, N_T, q_step, 0)
    for h in range(HEADS):
        cut = slice(h * 128, h * 128 + 128)
        for out, top in ((qp, 0), (qt, TOK)):
            z = qacc[pl.ds(top, TOK), cut]
            out[:, cut] = (z * cos_ref[...] + pltpu.roll(z, 64, 1) * sin_ref[...]).astype(bf16)

    for rel in PEERS:
        i = ridx(rel)
        arrived(kvr.at[source(me, rel)], kvs.at[i], kvrs.at[i])
    both = kvr[...].astype(f32)
    keys = both[:, 0:8, :].reshape(HEAD_DIM, 2 * TOK)
    vals = both[:, 8:16, :].reshape(HEAD_DIM, 2 * TOK).astype(bf16)
    vp[...] = vals[:, :TOK]
    vt[...] = vals[:, TOK:]
    cost, sint = cost_ref[...], sint_ref[...]
    for out, left in ((kp, 0), (kt, TOK)):
        z = keys[:, left : left + TOK]
        front, back = z[:64], z[64:]
        out[0:64, :] = (front * cost - back * sint).astype(bf16)
        out[64:128, :] = (back * cost + front * sint).astype(bf16)

    same = jnp.concatenate([docs[...], docs[...]], axis=1) == doc_ref[...].astype(f32)
    place = lax.broadcasted_iota(jnp.int32, (TOK, TOK), 0) >= lax.broadcasted_iota(jnp.int32, (TOK, TOK), 1)
    allowed = same & place
    score_scale = HEAD_DIM ** (-0.5)

    def dot(a, b):
        return jnp.dot(a, b, preferred_element_type=f32)

    for h in range(HEADS):
        cut = slice(h * 128, h * 128 + 128)
        q0, q1 = qp[:, cut], qt[:, cut]
        scores = jnp.where(allowed, dot(q0, kp[...]) * score_scale, MASKED)
        grown = jnp.exp(scores - jnp.max(scores, axis=1, keepdims=True))
        prob = grown / jnp.sum(grown, axis=1, keepdims=True)
        probs[h] = prob
        t = (dot(q1, kp[...]) + dot(q0, kt[...])) * score_scale
        tan = (prob * (t - jnp.sum(prob * t, axis=1, keepdims=True))).astype(bf16)
        ctx[:, cut] = (nt(tan, vp[...]) + nt(prob.astype(bf16), vt[...])).astype(bf16)

    loads[3].wait()
    order = CHIPS[::-1]

    def pair_part(s):
        dy, dz = order[s]
        pair_out[s] = dot(ctx[...], wo[:, lanes_of(peer(me, (dy, dz, 1)))]).astype(bf16)
        send(pair_out.at[s], pair_in.at[s], ps.at[s], pr.at[s], sibling)

    def own_part(s):
        dy, dz = order[s]
        to = peer(me, (dy, dz, 0))
        mine = dot(ctx[...], wo[:, lanes_of(to)]).astype(bf16).astype(f32)
        arrived(pair_in.at[s], ps.at[s], pr.at[s])
        part_out[s] = (mine + pair_in[s].astype(f32)).astype(bf16)
        if s < 7:
            send(part_out.at[s], part_in.at[s], qs.at[s], qr.at[s], to)

    pair_part(0)
    pair_part(1)
    for s in range(8):
        if s + 2 < 8:
            pair_part(s + 2)
        own_part(s)
    for s in range(7):
        arrived(part_in.at[s], qs.at[s], qr.at[s])

    def sum_step(r, carry):
        rows = pl.ds(pl.multiple_of(r * 32, 32), 32)
        value = part_out[7, rows, :].astype(f32)
        for s in range(7):
            value = value + part_in[s, rows, :].astype(f32)
        tg[me, rows, :] = value.astype(bf16)
        return carry

    lax.fori_loop(0, TOK // 32, sum_step, 0)
    send(tg.at[me], tg.at[me], gs.at[1], gr.at[1], sibling)
    for dy, dz in CHIPS[1:]:
        i = ridx((dy, dz, 0))
        send(tg.at[me], tg.at[me], gs.at[i], gr.at[i], peer(me, (dy, dz, 0)))
    out_ref[...] = tg[me]
    bacc[...] = jnp.zeros_like(bacc)

    def back(j):
        bacc[...] += nt(tg[j], wo[:, lanes_of(j)])

    gather(tg, gs, gr, gf, back)

    gk = jnp.zeros((HEAD_DIM, TOK), f32)
    gv = jnp.zeros((HEAD_DIM, TOK), f32)
    for h in range(HEADS):
        cut = slice(h * 128, h * 128 + 128)
        bc = bacc[:, cut].astype(bf16)
        prob = probs[h]
        g = dot(bc, vp[...])
        score = (prob * (g - jnp.sum(prob * g, axis=1, keepdims=True)) * score_scale).astype(bf16)
        z = nt(score, kp[...])
        gq[:, cut] = (z * cos_ref[...] - pltpu.roll(z, 64, 1) * sin_ref[...]).astype(bf16)
        gk = gk + tn(qp[:, cut], score)
        gv = gv + tn(bc, prob.astype(bf16))
    front, back_half = gk[:64], gk[64:]
    gk = jnp.concatenate([front * cost + back_half * sint, back_half * cost - front * sint], axis=0)
    gkv_out[...] = jnp.concatenate([gk.reshape(N_T, 8, TOK), gv.reshape(N_T, 8, TOK)], axis=1).astype(bf16)
    gkv_in[me] = gkv_out[me]
    for rel in PEERS:
        i = ridx(rel)
        to = peer(me, rel)
        send(gkv_out.at[to], gkv_in.at[me], ks.at[i], kr.at[i], to)

    def column_sums(product):
        line = jnp.sum(product, axis=0, keepdims=True)
        return jnp.concatenate([line[:, l * 128 : l * 128 + 128] for l in range(4)] * 2, axis=0)

    def query_step(j, carry):
        gnv[j] = column_sums(nt(gq[...], wq[lanes_of(j), :]) * slopes[j])
        return carry

    lax.fori_loop(0, N_T, query_step, 0)
    for rel in PEERS:
        i = ridx(rel)
        arrived(gkv_in.at[source(me, rel)], ks.at[i], kr.at[i])
    pairs = gkv_in[...].astype(f32).reshape(N_T // 2, 2, 16, TOK)
    summed = (pairs[:, 0] + pairs[:, 1]).reshape(HEAD_DIM, TOK).astype(bf16)
    gkv[...] = tn(summed, permutation()).astype(bf16)

    def key_step(j, carry):
        gnv[j] += column_sums(dot(gkv[...], wkv[:, lanes_of(j)]) * slopes[j])
        return carry

    lax.fori_loop(0, N_T, key_step, 0)
    gnv_in[me] = gnv[me]
    for rel in PEERS:
        i = ridx(rel)
        to = peer(me, rel)
        send(gnv.at[to], gnv_in.at[me], ns.at[i], nr.at[i], to)
    for rel in PEERS:
        i = ridx(rel)
        arrived(gnv_in.at[source(me, rel)], ns.at[i], nr.at[i])
    dpv[...] = jnp.sum(gnv_in[...], axis=0)
    dpv_in[dp] = dpv[...]
    for d in range(1, N_DP):
        send(dpv, dpv_in.at[dp], ds.at[d], dr.at[d], me, (dp + d) % N_DP)
    for d in range(1, N_DP):
        arrived(dpv_in.at[(dp + N_DP - d) % N_DP], ds.at[d], dr.at[d])
    gn_ref[...] = (jnp.sum(dpv_in[...], axis=0) / (TOK * N_DP))[0:4, :]
    for cp in sends:
        cp.wait_send()


VM = pl.BlockSpec(memory_space=pltpu.VMEM)
ANY = pl.BlockSpec(memory_space=pl.ANY)


def whole(*operands):
    sds = jax.ShapeDtypeStruct
    sem = pltpu.SemaphoreType.DMA((N_T,))
    vm = pltpu.VMEM
    return pl.pallas_call(
        body,
        name="block",
        out_shape=[sds((TOK, SHARD), bf16), sds((4, 128), f32)],
        in_specs=[VM] * 10 + [ANY] * 4,
        out_specs=[VM] * 2,
        scratch_shapes=[
            vm((N_T, TOK, SHARD), bf16),
            vm((N_T, 2 * TOK, SHARD), bf16),
            vm((N_T, TOK, SHARD), f32),
            vm((WIDTH, SHARD), bf16),
            vm((128, WIDTH), bf16),
            vm((SHARD, WIDTH), bf16),
            vm((8, TOK), f32),
            vm((N_T, 8, TOK), f32),
            vm((TOK, 128), f32),
            vm((2 * TOK, 128), f32),
            vm((2 * TOK, SHARD), f32),
            vm((128, 2 * TOK), bf16),
            vm((N_T, 16, 2 * TOK), bf16),
            vm((TOK, SHARD), bf16),
            vm((TOK, SHARD), bf16),
            vm((HEAD_DIM, TOK), bf16),
            vm((HEAD_DIM, TOK), bf16),
            vm((HEAD_DIM, TOK), bf16),
            vm((HEAD_DIM, TOK), bf16),
            vm((TOK, 128), f32),
            vm((HEADS, TOK, TOK), f32),
            vm((TOK, SHARD), bf16),
            vm((8, TOK, SHARD), bf16),
            vm((8, TOK, SHARD), bf16),
            vm((8, TOK, SHARD), bf16),
            vm((8, TOK, SHARD), bf16),
            vm((N_T, TOK, SHARD), bf16),
            vm((TOK, SHARD), f32),
            vm((TOK, SHARD), bf16),
            vm((N_T, 16, TOK), bf16),
            vm((N_T, 16, TOK), bf16),
            vm((TOK, 128), bf16),
            vm((N_T, 8, 128), f32),
            vm((N_T, 8, 128), f32),
            vm((8, 128), f32),
            vm((N_DP, 8, 128), f32),
            pltpu.SemaphoreType.DMA((4,)),
        ]
        + [sem] * 20,
        compiler_params=pltpu.CompilerParams(collective_id=1, has_side_effects=True, vmem_limit_bytes=VMEM_BYTES),
    )(*operands)


def tables():
    positions = np.arange(TOK, dtype=np.float32)
    frequency = np.exp(np.float32(-math.log(ROPE_BASE) * 2.0) * np.arange(64, dtype=np.float32) / np.float32(HEAD_DIM))
    angles = positions[:, None] * frequency[None, :].astype(np.float32)
    cosine, sine = np.cos(angles), np.sin(angles)
    return (
        np.concatenate([cosine, cosine], axis=1),
        np.concatenate([-sine, sine], axis=1),
        np.ascontiguousarray(cosine.T),
        np.ascontiguousarray(sine.T),
    )


def on_device(
    hidden_in, norm_gain, clip_base, pct_index, clip_step, w_query, w_key, w_value, w_out, doc_ids
):
    row = lambda v: v.reshape(1, WIDTH)
    tangent_shard, gn = whole(
        hidden_in, row(norm_gain), row(clip_base), row(pct_index), row(clip_step), doc_ids,
        *(jnp.asarray(t) for t in tables()),
        w_query, w_key.T, w_value.T, w_out,
    )
    return (tangent_shard, gn.reshape(SHARD))


def solution(mesh):
    in_specs = (
        P("dp", "tensor"),
        P(),
        P(),
        P(),
        P(),
        P(None, "tensor"),
        P(None, "tensor"),
        P(None, "tensor"),
        P("tensor", None),
        P("dp", None),
    )
    out_specs = (P("dp", "tensor"), P("tensor"))
    return jax.shard_map(
        on_device, mesh=mesh, in_specs=in_specs, out_specs=out_specs, check_vma=False
    )
```

```python
import functools
import math

import jax
import jax.numpy as jnp
import numpy as np
from jax import lax
from jax.experimental import pallas as pl
from jax.experimental.pallas import tpu as pltpu
from jax.sharding import PartitionSpec as P

HEAD_DIM = 128
EPSILON = 1e-05
ROPE_BASE = 500000.0
MASKED = -1e30
MESH = pl.DeviceIdType.MESH
f32 = jnp.float32
bf16 = jnp.bfloat16

N_Y, N_Z, N_C = 2, 4, 2
N_T = N_Y * N_Z * N_C
TOK = 256
SHARD = 512
WIDTH = N_T * SHARD
HEADS = 4
N_DP = 8
VMEM_BYTES = 60 << 20

RELS = [(dy, dz, dc) for dy in range(N_Y) for dz in range(N_Z) for dc in range(N_C)]
PEERS = [r for r in RELS if r != (0, 0, 0)]
ROWS = {"A": (0, 128), "B": (128, 128), "0": (0, 64), "1": (64, 64), "2": (128, 64), "3": (192, 64)}
Y, ZP, ZM = (1, 0), (0, 1), (0, 3)

MOVES = [
    ((0, 0), "B", Y), ((0, 0), "A", Y), ((0, 0), "A", ZP), ((0, 0), "A", ZM), ((0, 0), "B", ZP), ((0, 0), "B", ZM),
    ((0, 3), "0", ZP), ((0, 1), "1", ZM), ((0, 3), "2", ZP), ((0, 1), "3", ZM), ((0, 3), "A", Y), ((0, 1), "A", Y),
    ((1, 0), "B", ZP), ((1, 0), "B", ZM), ((1, 3), "2", ZP), ((1, 1), "3", ZM), ((0, 2), "0", Y), ((0, 2), "1", Y),
]
EVENTS = [
    ([0], [12, 13], [((1, 0), 1)]),
    ([2], [10, 6], [((0, 3), 0)]),
    ([3], [11, 7], [((0, 1), 0)]),
    ([1], [], [((1, 0), 0)]),
    ([4], [8], [((0, 3), 1)]),
    ([5], [9], [((0, 1), 1)]),
    ([6, 7], [16, 17], [((0, 2), 0)]),
    ([12, 13], [14, 15], [((1, 3), 1), ((1, 1), 1)]),
    ([8, 9], [], [((0, 2), 1)]),
    ([10, 11], [], [((1, 3), 0), ((1, 1), 0)]),
    ([14, 15], [], [((1, 2), 1)]),
    ([16, 17], [], [((1, 2), 0)]),
]
SUMS = [
    ((1, 2), "A", Y), ((1, 1), "A", Y), ((1, 3), "A", Y), ((1, 2), "2", ZM), ((1, 2), "3", ZP),
    ((0, 2), "0", ZM), ((0, 2), "1", ZP), ((0, 2), "2", ZM), ((0, 2), "3", ZP), ((1, 1), "B", ZP), ((1, 3), "B", ZM),
    ((1, 0), "A", Y), ((1, 0), "B", Y), ((0, 1), "A", ZP), ((0, 3), "A", ZM), ((0, 1), "B", ZP), ((0, 3), "B", ZM),
]
PARTS = [(1, 2), (1, 1), (1, 3), (0, 2), (1, 0), (0, 1), (0, 3), (0, 0)]
FIRST = {(1, 2): [0, 3, 4], (1, 1): [1], (1, 3): [2], (0, 2): [7, 8], (1, 0): [11]}


def minus(a, b):
    return ((a[0] - b[0]) % N_Y, (a[1] - b[1]) % N_Z)


def ridx(rel):
    return (rel[0] * N_Z + rel[1]) * N_C + rel[2]


def peer(me, rel):
    y, z, c = me // (N_Z * N_C), (me // N_C) % N_Z, me % N_C
    y = (y + rel[0]) % N_Y
    z = (z + rel[1]) % N_Z
    c = (c + rel[2]) % N_C
    return (y * N_Z + z) * N_C + c


def source(me, rel):
    return peer(me, (-rel[0], -rel[1], -rel[2]))


def remote(src, dst, ssem, rsem, dp, target):
    return pltpu.make_async_remote_copy(
        src_ref=src, dst_ref=dst, send_sem=ssem, recv_sem=rsem, device_id=(dp, target), device_id_type=MESH
    )


def nt(a, b):
    return lax.dot_general(a, b, (((1,), (1,)), ((), ())), preferred_element_type=f32)


def tn(a, b):
    return lax.dot_general(a, b, (((0,), (0,)), ((), ())), preferred_element_type=f32)


def permutation():
    row = lax.broadcasted_iota(jnp.int32, (128, 128), 0)
    col = lax.broadcasted_iota(jnp.int32, (128, 128), 1)
    head, low = row // 16, row % 16
    want = jnp.where(low < 8, low * 8 + head, 64 + (low - 8) * 8 + head)
    return (col == want).astype(f32).astype(bf16)


def body(
    x_ref, gain_ref, base_ref, pct_ref, step_ref, doc_ref, cos_ref, sin_ref, cost_ref, sint_ref,
    wq_hbm, wk_hbm, wv_hbm, wo_hbm,
    out_ref, gn_ref,
    hid, xs, slopes, wq, wkv, wo, ss_send, ssr, rs, kvacc, qacc, kvt, kvr, qp, qt, kp, kt, vp, vt, docs, probs, ctx,
    pair_out, pair_in, part, sums, tg, bacc, gq, gkv_out, gkv_in, gkv, gnv, gnv_in, dpv, dpv_in,
    wsem, hs, hr, hfs, hfr, sss, ssrs, kvs, kvrs, ps, pr, qs, qr, gs, gr, gfs, gfr, ks, kr, ns, nr, ds, dr,
):
    me = lax.axis_index("tensor")
    dp = lax.axis_index("dp")
    sibling = peer(me, (0, 0, 1))
    barrier = pltpu.get_barrier_semaphore()
    for rel in PEERS:
        pl.semaphore_signal(barrier, inc=1, device_id=(dp, peer(me, rel)), device_id_type=MESH)
    for d in range(1, N_DP):
        pl.semaphore_signal(barrier, inc=1, device_id=((dp + d) % N_DP, me), device_id_type=MESH)
    loads = [
        pltpu.make_async_copy(wk_hbm, wkv.at[pl.ds(0, 64)], wsem.at[0]),
        pltpu.make_async_copy(wv_hbm, wkv.at[pl.ds(64, 64)], wsem.at[1]),
        pltpu.make_async_copy(wq_hbm, wq, wsem.at[2]),
        pltpu.make_async_copy(wo_hbm, wo, wsem.at[3]),
    ]
    for load in loads:
        load.start()

    sends = []

    def send(src, dst, ssem, rsem, to, group=None):
        cp = remote(src, dst, ssem, rsem, dp if group is None else group, to)
        cp.start()
        sends.append(cp)

    def arrived(dst, ssem, rsem):
        remote(dst, dst, ssem, rsem, dp, me).wait_recv()

    own = x_ref[...].astype(f32)
    square = own * own
    high = square.astype(bf16)
    low = (square - high.astype(f32)).astype(bf16)
    ones = jnp.ones((8, SHARD), bf16)
    ss_send[...] = nt(ones, high) + nt(ones, low)
    ssr[me] = ss_send[...]
    hid[me] = x_ref[...]
    docs[...] = jnp.transpose(jnp.broadcast_to(doc_ref[...].astype(f32), (128, TOK)))

    pl.semaphore_wait(barrier, len(PEERS) + N_DP - 1)
    for rel in PEERS:
        i = ridx(rel)
        send(ss_send, ssr.at[me], sss.at[i], ssrs.at[i], peer(me, rel))

    def piece(buf, owner, rows):
        start, size = ROWS[rows]
        return buf.at[peer(me, owner + (0,)), pl.ds(start, size)]

    def move(buf, ssem, rsem, k):
        owner, rows, way = MOVES[k]
        ref = piece(buf, owner, rows)
        send(ref, ref, ssem.at[k], rsem.at[k], peer(me, way + (0,)))

    def moved(buf, ssem, rsem, k):
        owner, rows, way = MOVES[k]
        arrived(piece(buf, minus(owner, way), rows), ssem.at[k], rsem.at[k])

    def forward(buf, ssem, rsem, owner, half):
        i = (owner[0] * N_Z + owner[1]) * 2 + half
        ref = piece(buf, owner, "AB"[half])
        send(ref, ref, ssem.at[i], rsem.at[i], sibling)

    def gather(buf, ssem, rsem, fssem, frsem, use_half, use_block):
        ready = [((0, 0), c, h) for c in range(N_C) for h in range(2)]
        done = set()

        def run(count):
            for owner, core, half in ready[:count]:
                j = peer(me, owner + (core,))
                if core == 1:
                    i = (owner[0] * N_Z + owner[1]) * 2 + half
                    arrived(buf.at[j, pl.ds(half * 128, 128)], fssem.at[i], frsem.at[i])
                use_half(j, half)
                done.add((owner, core, half))
                if (owner, core, 1 - half) in done:
                    use_block(j)
            del ready[:count]

        for waits, starts, halves in EVENTS:
            for k in waits:
                moved(buf, ssem, rsem, k)
            for k in starts:
                move(buf, ssem, rsem, k)
            for owner, half in halves:
                forward(buf, fssem, frsem, owner, half)
            run(2 * len(halves))
            ready += [(owner, core, half) for core in range(N_C) for owner, half in halves]
        run(len(ready))

    for half, starts in ((1, (0, 4, 5)), (0, (1, 2, 3))):
        for k in starts:
            move(hid, hs, hr, k)
        forward(hid, hfs, hfr, (0, 0), half)
    for rel in PEERS:
        i = ridx(rel)
        arrived(ssr.at[source(me, rel)], sss.at[i], ssrs.at[i])
    total = jnp.sum(ssr[...], axis=0)
    scale = lax.rsqrt(total / WIDTH + EPSILON)
    rs[...] = jnp.transpose(jnp.broadcast_to(scale[0:1, :], (128, TOK)))

    kvacc[...] = jnp.zeros_like(kvacc)

    def lanes_of(j):
        return pl.ds(pl.multiple_of(j * SHARD, SHARD), SHARD)

    def clip(j, half):
        lanes = lanes_of(j)
        thresh = base_ref[:, lanes] * (1.0 + pct_ref[:, lanes].astype(f32) / 32.0)
        over = gain_ref[:, lanes] / thresh
        step = step_ref[:, lanes]

        def rows_step(r, carry):
            rows = pl.ds(pl.multiple_of(half * 128 + r * 32, 32), 32)
            near = pl.ds(pl.multiple_of(half * 256 + r * 32, 32), 32)
            rest = pl.ds(pl.multiple_of(half * 256 + 128 + r * 32, 32), 32)
            x = hid[j, rows, :].astype(f32)
            scale = rs[rows, :]
            for l in range(SHARD // 128):
                cut = slice(l * 128, l * 128 + 128)
                ratio = x[:, cut] * scale * over[:, cut]
                bent = jnp.tanh(ratio)
                xs[j, near, cut] = (thresh[:, cut] * bent).astype(bf16)
                slope = bent - ratio * (1.0 - bent * bent)
                slopes[j, rows, cut] = slope
                xs[j, rest, cut] = (slope * step[:, cut]).astype(bf16)
            return carry

        lax.fori_loop(0, 4, rows_step, 0)

    def project(j):
        kvacc[...] += nt(xs[j], wkv[:, lanes_of(j)])

    loads[0].wait()
    loads[1].wait()

    gather(hid, hs, hr, hfs, hfr, clip, project)

    kvt[...] = nt(permutation(), kvacc[...].astype(bf16)).astype(bf16)

    def block(chip):
        return pl.ds(pl.multiple_of(chip * 16, 16), 16)

    kvr[me] = kvt[block(me // N_C), :]
    for rel in PEERS:
        i = ridx(rel)
        to = peer(me, rel)
        send(kvt.at[block(to // N_C)], kvr.at[me], kvs.at[i], kvrs.at[i], to)

    loads[2].wait()
    qacc[...] = jnp.zeros_like(qacc)

    def q_step(j, carry):
        qacc[...] += jnp.dot(xs[j], wq[lanes_of(j), :], preferred_element_type=f32)
        return carry

    lax.fori_loop(0, N_T, q_step, 0)
    for h in range(HEADS):
        cut = slice(h * 128, h * 128 + 128)
        for half in range(2):
            rows = pl.ds(half * 128, 128)
            for out, top in ((qp, 0), (qt, 128)):
                z = qacc[pl.ds(half * 256 + top, 128), cut]
                out[rows, cut] = (z * cos_ref[rows, :] + pltpu.roll(z, 64, 1) * sin_ref[rows, :]).astype(bf16)

    for rel in PEERS:
        i = ridx(rel)
        arrived(kvr.at[source(me, rel)], kvs.at[i], kvrs.at[i])
    both = kvr[...].astype(f32)
    keys = both[:, 0:8, :].reshape(HEAD_DIM, 2 * TOK)
    vals = both[:, 8:16, :].reshape(HEAD_DIM, 2 * TOK).astype(bf16)
    for half in range(2):
        vp[:, half * 128 : half * 128 + 128] = vals[:, half * 256 : half * 256 + 128]
        vt[:, half * 128 : half * 128 + 128] = vals[:, half * 256 + 128 : half * 256 + 256]
    cost, sint = cost_ref[...], sint_ref[...]
    for out, left in ((kp, 0), (kt, 128)):
        z = jnp.concatenate([keys[:, left : left + 128], keys[:, left + 256 : left + 384]], axis=1)
        front, back = z[:64], z[64:]
        out[0:64, :] = (front * cost - back * sint).astype(bf16)
        out[64:128, :] = (back * cost + front * sint).astype(bf16)

    same = jnp.concatenate([docs[...], docs[...]], axis=1) == doc_ref[...].astype(f32)
    place = lax.broadcasted_iota(jnp.int32, (TOK, TOK), 0) >= lax.broadcasted_iota(jnp.int32, (TOK, TOK), 1)
    allowed = same & place
    score_scale = HEAD_DIM ** (-0.5)

    def dot(a, b):
        return jnp.dot(a, b, preferred_element_type=f32)

    for h in range(HEADS):
        cut = slice(h * 128, h * 128 + 128)
        q0, q1 = qp[:, cut], qt[:, cut]
        scores = jnp.where(allowed, dot(q0, kp[...]) * score_scale, MASKED)
        grown = jnp.exp(scores - jnp.max(scores, axis=1, keepdims=True))
        prob = grown / jnp.sum(grown, axis=1, keepdims=True)
        probs[h] = prob
        t = (dot(q1, kp[...]) + dot(q0, kt[...])) * score_scale
        tan = (prob * (t - jnp.sum(prob * t, axis=1, keepdims=True))).astype(bf16)
        ctx[:, cut] = (nt(tan, vp[...]) + nt(prob.astype(bf16), vt[...])).astype(bf16)

    loads[3].wait()

    def slot(chip):
        return chip[0] * N_Z + chip[1]

    def pair_part(s):
        i = slot(PARTS[s])
        pair_out[i] = dot(ctx[...], wo[:, lanes_of(peer(me, PARTS[s] + (1,)))]).astype(bf16)
        send(pair_out.at[i], pair_in.at[i], ps.at[i], pr.at[i], sibling)

    def give(k):
        chip, rows, way = SUMS[k]
        start, size = ROWS[rows]
        send(part.at[slot(chip), pl.ds(start, size)], sums.at[k, pl.ds(0, size)], qs.at[k], qr.at[k], peer(me, way + (0,)))

    def own_part(s):
        i = slot(PARTS[s])
        mine = dot(ctx[...], wo[:, lanes_of(peer(me, PARTS[s] + (0,)))]).astype(bf16).astype(f32)
        arrived(pair_in.at[i], ps.at[i], pr.at[i])
        part[i] = (mine + pair_in[i].astype(f32)).astype(bf16)
        for k in FIRST.get(PARTS[s], ()):
            give(k)

    def add(rows, into, *parts):
        chip, out = into
        start, size = ROWS[rows]
        for k in parts:
            arrived(sums.at[k, pl.ds(0, ROWS[SUMS[k][1]][1])], qs.at[k], qr.at[k])
        value = part[slot(chip), pl.ds(start, size), :].astype(f32)
        for k in parts:
            low = start - ROWS[SUMS[k][1]][0]
            value = value + sums[k, pl.ds(low, size), :].astype(f32)
        if out is None:
            part[slot(chip), pl.ds(start, size), :] = value.astype(bf16)
        else:
            out[me, pl.ds(start, size), :] = value.astype(bf16)

    def take(rows, chip, *parts):
        add(rows, (chip, None), *parts)

    pair_part(0)
    pair_part(1)
    for s in range(8):
        if s + 2 < 8:
            pair_part(s + 2)
        own_part(s)
        if s == 5:
            take("2", (1, 3), 3)
            give(10)
            take("3", (1, 1), 4)
            give(9)
    take("A", (0, 2), 0)
    give(5)
    give(6)
    take("2", (0, 3), 7)
    give(16)
    take("3", (0, 1), 8)
    give(15)
    take("B", (1, 0), 9, 10)
    give(12)
    take("1", (0, 1), 6)
    take("A", (0, 1), 1)
    give(13)
    take("0", (0, 3), 5)
    take("A", (0, 3), 2)
    give(14)
    add("B", ((0, 0), tg), 12, 15, 16)
    for k in (0, 4, 5):
        move(tg, gs, gr, k)
    forward(tg, gfs, gfr, (0, 0), 1)
    add("A", ((0, 0), tg), 11, 13, 14)
    for k in (1, 2, 3):
        move(tg, gs, gr, k)
    forward(tg, gfs, gfr, (0, 0), 0)
    out_ref[...] = tg[me]
    bacc[...] = jnp.zeros_like(bacc)

    def back(j):
        bacc[...] += nt(tg[j], wo[:, lanes_of(j)])

    gather(tg, gs, gr, gfs, gfr, lambda j, half: None, back)

    gk = jnp.zeros((HEAD_DIM, TOK), f32)
    gv = jnp.zeros((HEAD_DIM, TOK), f32)
    for h in range(HEADS):
        cut = slice(h * 128, h * 128 + 128)
        bc = bacc[:, cut].astype(bf16)
        prob = probs[h]
        g = dot(bc, vp[...])
        score = (prob * (g - jnp.sum(prob * g, axis=1, keepdims=True)) * score_scale).astype(bf16)
        z = nt(score, kp[...])
        gq[:, cut] = (z * cos_ref[...] - pltpu.roll(z, 64, 1) * sin_ref[...]).astype(bf16)
        gk = gk + tn(qp[:, cut], score)
        gv = gv + tn(bc, prob.astype(bf16))
    front, back_half = gk[:64], gk[64:]
    gk = jnp.concatenate([front * cost + back_half * sint, back_half * cost - front * sint], axis=0)
    gkv_out[...] = jnp.concatenate([gk.reshape(N_T, 8, TOK), gv.reshape(N_T, 8, TOK)], axis=1).astype(bf16)
    gkv_in[me] = gkv_out[me]
    for rel in PEERS:
        i = ridx(rel)
        to = peer(me, rel)
        send(gkv_out.at[to], gkv_in.at[me], ks.at[i], kr.at[i], to)

    def column_sums(product):
        line = jnp.sum(product, axis=0, keepdims=True)
        return jnp.concatenate([line[:, l * 128 : l * 128 + 128] for l in range(4)] * 2, axis=0)

    def query_step(j, carry):
        gnv[j] = column_sums(nt(gq[...], wq[lanes_of(j), :]) * slopes[j])
        return carry

    lax.fori_loop(0, N_T, query_step, 0)
    for rel in PEERS:
        i = ridx(rel)
        arrived(gkv_in.at[source(me, rel)], ks.at[i], kr.at[i])
    pairs = gkv_in[...].astype(f32).reshape(N_T // 2, 2, 16, TOK)
    summed = (pairs[:, 0] + pairs[:, 1]).reshape(HEAD_DIM, TOK).astype(bf16)
    gkv[...] = tn(summed, permutation()).astype(bf16)

    def key_step(j, carry):
        gnv[j] += column_sums(dot(gkv[...], wkv[:, lanes_of(j)]) * slopes[j])
        return carry

    lax.fori_loop(0, N_T, key_step, 0)
    gnv_in[me] = gnv[me]
    for rel in PEERS:
        i = ridx(rel)
        to = peer(me, rel)
        send(gnv.at[to], gnv_in.at[me], ns.at[i], nr.at[i], to)
    for rel in PEERS:
        i = ridx(rel)
        arrived(gnv_in.at[source(me, rel)], ns.at[i], nr.at[i])
    dpv[...] = jnp.sum(gnv_in[...], axis=0)
    dpv_in[dp] = dpv[...]
    for d in range(1, N_DP):
        send(dpv, dpv_in.at[dp], ds.at[d], dr.at[d], me, (dp + d) % N_DP)
    for d in range(1, N_DP):
        arrived(dpv_in.at[(dp + N_DP - d) % N_DP], ds.at[d], dr.at[d])
    gn_ref[...] = (jnp.sum(dpv_in[...], axis=0) / (TOK * N_DP))[0:4, :]
    for cp in sends:
        cp.wait_send()


VM = pl.BlockSpec(memory_space=pltpu.VMEM)
ANY = pl.BlockSpec(memory_space=pl.ANY)


def whole(*operands):
    sds = jax.ShapeDtypeStruct
    sem = pltpu.SemaphoreType.DMA((18,))
    vm = pltpu.VMEM
    return pl.pallas_call(
        body,
        name="block",
        out_shape=[sds((TOK, SHARD), bf16), sds((4, 128), f32)],
        in_specs=[VM] * 10 + [ANY] * 4,
        out_specs=[VM] * 2,
        scratch_shapes=[
            vm((N_T, TOK, SHARD), bf16),
            vm((N_T, 2 * TOK, SHARD), bf16),
            vm((N_T, TOK, SHARD), f32),
            vm((WIDTH, SHARD), bf16),
            vm((128, WIDTH), bf16),
            vm((SHARD, WIDTH), bf16),
            vm((8, TOK), f32),
            vm((N_T, 8, TOK), f32),
            vm((TOK, 128), f32),
            vm((2 * TOK, 128), f32),
            vm((2 * TOK, SHARD), f32),
            vm((128, 2 * TOK), bf16),
            vm((N_T, 16, 2 * TOK), bf16),
            vm((TOK, SHARD), bf16),
            vm((TOK, SHARD), bf16),
            vm((HEAD_DIM, TOK), bf16),
            vm((HEAD_DIM, TOK), bf16),
            vm((HEAD_DIM, TOK), bf16),
            vm((HEAD_DIM, TOK), bf16),
            vm((TOK, 128), f32),
            vm((HEADS, TOK, TOK), f32),
            vm((TOK, SHARD), bf16),
            vm((8, TOK, SHARD), bf16),
            vm((8, TOK, SHARD), bf16),
            vm((8, TOK, SHARD), bf16),
            vm((len(SUMS), 128, SHARD), bf16),
            vm((N_T, TOK, SHARD), bf16),
            vm((TOK, SHARD), f32),
            vm((TOK, SHARD), bf16),
            vm((N_T, 16, TOK), bf16),
            vm((N_T, 16, TOK), bf16),
            vm((TOK, 128), bf16),
            vm((N_T, 8, 128), f32),
            vm((N_T, 8, 128), f32),
            vm((8, 128), f32),
            vm((N_DP, 8, 128), f32),
            pltpu.SemaphoreType.DMA((4,)),
        ]
        + [sem] * 22,
        compiler_params=pltpu.CompilerParams(collective_id=1, has_side_effects=True, vmem_limit_bytes=VMEM_BYTES),
    )(*operands)


def tables():
    positions = np.arange(TOK, dtype=np.float32)
    frequency = np.exp(np.float32(-math.log(ROPE_BASE) * 2.0) * np.arange(64, dtype=np.float32) / np.float32(HEAD_DIM))
    angles = positions[:, None] * frequency[None, :].astype(np.float32)
    cosine, sine = np.cos(angles), np.sin(angles)
    return (
        np.concatenate([cosine, cosine], axis=1),
        np.concatenate([-sine, sine], axis=1),
        np.ascontiguousarray(cosine.T),
        np.ascontiguousarray(sine.T),
    )


def on_device(
    hidden_in, norm_gain, clip_base, pct_index, clip_step, w_query, w_key, w_value, w_out, doc_ids
):
    row = lambda v: v.reshape(1, WIDTH)
    tangent_shard, gn = whole(
        hidden_in, row(norm_gain), row(clip_base), row(pct_index), row(clip_step), doc_ids,
        *(jnp.asarray(t) for t in tables()),
        w_query, w_key.T, w_value.T, w_out,
    )
    return (tangent_shard, gn.reshape(SHARD))


def solution(mesh):
    in_specs = (
        P("dp", "tensor"),
        P(),
        P(),
        P(),
        P(),
        P(None, "tensor"),
        P(None, "tensor"),
        P(None, "tensor"),
        P("tensor", None),
        P("dp", None),
    )
    out_specs = (P("dp", "tensor"), P("tensor"))
    return jax.shard_map(
        on_device, mesh=mesh, in_specs=in_specs, out_specs=out_specs, check_vma=False
    )
```

```python
import functools
import math

import jax
import jax.numpy as jnp
import numpy as np
from jax import lax
from jax.experimental import pallas as pl
from jax.experimental.pallas import tpu as pltpu
from jax.sharding import PartitionSpec as P

HEAD_DIM = 128
EPSILON = 1e-05
ROPE_BASE = 500000.0
MASKED = -1e30
MESH = pl.DeviceIdType.MESH
f32 = jnp.float32
bf16 = jnp.bfloat16

N_Y, N_Z, N_C = 2, 4, 2
N_T = N_Y * N_Z * N_C
TOK = 256
SHARD = 512
WIDTH = N_T * SHARD
HEADS = 4
N_DP = 8
VMEM_BYTES = 60 << 20
LATE = 16

RELS = [(dy, dz, dc) for dy in range(N_Y) for dz in range(N_Z) for dc in range(N_C)]
PEERS = [r for r in RELS if r != (0, 0, 0)]
ROWS = {"A": (0, 128), "B": (128, 128), "0": (0, 64), "1": (64, 64), "2": (128, 64), "3": (192, 64)}
Y, ZP, ZM = (1, 0), (0, 1), (0, 3)

MOVES = [
    ((0, 0), "B", Y), ((0, 0), "A", Y), ((0, 0), "A", ZP), ((0, 0), "A", ZM), ((0, 0), "B", ZP), ((0, 0), "B", ZM),
    ((0, 3), "0", ZP), ((0, 1), "1", ZM), ((0, 3), "2", ZP), ((0, 1), "3", ZM), ((0, 3), "A", Y), ((0, 1), "A", Y),
    ((1, 0), "B", ZP), ((1, 0), "B", ZM), ((1, 3), "2", ZP), ((1, 1), "3", ZM), ((0, 2), "0", Y), ((0, 2), "1", Y),
]
EVENTS = [
    ([0], [12, 13], [((1, 0), 1)]),
    ([2], [10, 6], [((0, 3), 0)]),
    ([3], [11, 7], [((0, 1), 0)]),
    ([1], [], [((1, 0), 0)]),
    ([4], [8], [((0, 3), 1)]),
    ([5], [9], [((0, 1), 1)]),
    ([6, 7], [16, 17], [((0, 2), 0)]),
    ([12, 13], [14, 15], [((1, 3), 1), ((1, 1), 1)]),
    ([8, 9], [], [((0, 2), 1)]),
    ([10, 11], [], [((1, 3), 0), ((1, 1), 0)]),
    ([14, 15], [], [((1, 2), 1)]),
    ([16, 17], [], [((1, 2), 0)]),
]
SUMS = [
    ((1, 2), "A", Y), ((1, 1), "A", Y), ((1, 3), "A", Y), ((1, 2), "2", ZM), ((1, 2), "3", ZP),
    ((0, 2), "0", ZM), ((0, 2), "1", ZP), ((0, 2), "2", ZM), ((0, 2), "3", ZP), ((1, 1), "B", ZP), ((1, 3), "B", ZM),
    ((1, 0), "A", Y), ((1, 0), "B", Y), ((0, 1), "A", ZP), ((0, 3), "A", ZM), ((0, 1), "B", ZP), ((0, 3), "B", ZM),
]
PARTS = [(1, 2), (1, 1), (1, 3), (0, 2), (1, 0), (0, 1), (0, 3), (0, 0)]
FIRST = {(1, 2): [0, 3, 4], (1, 1): [1], (1, 3): [2], (0, 2): [7, 8], (1, 0): [11]}


def minus(a, b):
    return ((a[0] - b[0]) % N_Y, (a[1] - b[1]) % N_Z)


def ridx(rel):
    return (rel[0] * N_Z + rel[1]) * N_C + rel[2]


def peer(me, rel):
    y, z, c = me // (N_Z * N_C), (me // N_C) % N_Z, me % N_C
    y = (y + rel[0]) % N_Y
    z = (z + rel[1]) % N_Z
    c = (c + rel[2]) % N_C
    return (y * N_Z + z) * N_C + c


def source(me, rel):
    return peer(me, (-rel[0], -rel[1], -rel[2]))


def remote(src, dst, ssem, rsem, dp, target):
    return pltpu.make_async_remote_copy(
        src_ref=src, dst_ref=dst, send_sem=ssem, recv_sem=rsem, device_id=(dp, target), device_id_type=MESH
    )


def nt(a, b):
    return lax.dot_general(a, b, (((1,), (1,)), ((), ())), preferred_element_type=f32)


def tn(a, b):
    return lax.dot_general(a, b, (((0,), (0,)), ((), ())), preferred_element_type=f32)


def permutation():
    row = lax.broadcasted_iota(jnp.int32, (128, 128), 0)
    col = lax.broadcasted_iota(jnp.int32, (128, 128), 1)
    head, low = row // 16, row % 16
    want = jnp.where(low < 8, low * 8 + head, 64 + (low - 8) * 8 + head)
    return (col == want).astype(f32).astype(bf16)


def body(
    x_hbm, gain_hbm, base_hbm, pct_hbm, step_hbm, doc_hbm, cos_hbm, sin_hbm, cost_hbm, sint_hbm,
    wq_hbm, wk_hbm, wv_hbm, wo_hbm,
    out_hbm, gn_ref,
    gain_ref, base_ref, pct_ref, step_ref, doc_ref, cos_ref, sin_ref, cost_ref, sint_ref,
    hid, xs, slopes, wq, wkv, wo, ss_send, ssr, rs, kvacc, qacc, kvt, kvr, qp, qt, kp, kt, vp, vt, docs, probs, ctx,
    pair_out, pair_in, part, sums, tg, bacc, gq, gkv_out, gkv_in, gkv, gnv, gnv_in, dpv, dpv_in,
    wsem, hs, hr, hfs, hfr, sss, ssrs, kvs, kvrs, ps, pr, qs, qr, gs, gr, gfs, gfr, ks, kr, ns, nr, ds, dr,
):
    me = lax.axis_index("tensor")
    dp = lax.axis_index("dp")
    sibling = peer(me, (0, 0, 1))
    barrier = pltpu.get_barrier_semaphore()
    for rel in PEERS:
        pl.semaphore_signal(barrier, inc=1, device_id=(dp, peer(me, rel)), device_id_type=MESH)
    for d in range(1, N_DP):
        pl.semaphore_signal(barrier, inc=1, device_id=((dp + d) % N_DP, me), device_id_type=MESH)
    copies = [
        (x_hbm, hid.at[me]), (doc_hbm, doc_ref), (gain_hbm, gain_ref), (base_hbm, base_ref), (pct_hbm, pct_ref),
        (step_hbm, step_ref), (cos_hbm, cos_ref), (sin_hbm, sin_ref), (cost_hbm, cost_ref), (sint_hbm, sint_ref),
    ]
    small = [pltpu.make_async_copy(a, b, wsem.at[4 + i]) for i, (a, b) in enumerate(copies)]
    for load in small:
        load.start()
    loads = [
        pltpu.make_async_copy(wk_hbm, wkv.at[pl.ds(0, 64)], wsem.at[0]),
        pltpu.make_async_copy(wv_hbm, wkv.at[pl.ds(64, 64)], wsem.at[1]),
        pltpu.make_async_copy(wq_hbm, wq, wsem.at[2]),
        pltpu.make_async_copy(wo_hbm, wo, wsem.at[3]),
    ]
    for load in loads:
        load.start()

    sends = []

    def send(src, dst, ssem, rsem, to, group=None):
        cp = remote(src, dst, ssem, rsem, dp if group is None else group, to)
        cp.start()
        sends.append(cp)

    def arrived(dst, ssem, rsem):
        remote(dst, dst, ssem, rsem, dp, me).wait_recv()

    small[0].wait()
    own = hid[me].astype(f32)
    square = own * own
    high = square.astype(bf16)
    low = (square - high.astype(f32)).astype(bf16)
    ones = jnp.ones((8, SHARD), bf16)
    ss_send[...] = nt(ones, high) + nt(ones, low)
    ssr[me] = ss_send[...]
    for load in small[1:]:
        load.wait()
    docs[...] = jnp.transpose(jnp.broadcast_to(doc_ref[...].astype(f32), (128, TOK)))

    pl.semaphore_wait(barrier, len(PEERS) + N_DP - 1)
    for rel in PEERS:
        i = ridx(rel)
        send(ss_send, ssr.at[me], sss.at[i], ssrs.at[i], peer(me, rel))

    def piece(buf, owner, rows):
        start, size = ROWS[rows]
        return buf.at[peer(me, owner + (0,)), pl.ds(start, size)]

    def move(buf, ssem, rsem, k):
        owner, rows, way = MOVES[k]
        ref = piece(buf, owner, rows)
        send(ref, ref, ssem.at[k], rsem.at[k], peer(me, way + (0,)))

    def moved(buf, ssem, rsem, k):
        owner, rows, way = MOVES[k]
        arrived(piece(buf, minus(owner, way), rows), ssem.at[k], rsem.at[k])

    def forward(buf, ssem, rsem, owner, half):
        i = (owner[0] * N_Z + owner[1]) * 2 + half
        ref = piece(buf, owner, "AB"[half])
        send(ref, ref, ssem.at[i], rsem.at[i], sibling)

    def gather(buf, ssem, rsem, fssem, frsem, use_half, use_block, before):
        ready = [((0, 0), c, h) for c in range(N_C) for h in range(2)]
        done = set()

        def run(count):
            for owner, core, half in ready[:count]:
                j = peer(me, owner + (core,))
                if core == 1:
                    i = (owner[0] * N_Z + owner[1]) * 2 + half
                    arrived(buf.at[j, pl.ds(half * 128, 128)], fssem.at[i], frsem.at[i])
                use_half(j, half)
                done.add((owner, core, half))
                if (owner, core, 1 - half) in done:
                    use_block(j)
            del ready[:count]

        for step, (waits, starts, halves) in enumerate(EVENTS):
            for k in waits:
                moved(buf, ssem, rsem, k)
            for k in starts:
                move(buf, ssem, rsem, k)
            for owner, half in halves:
                forward(buf, fssem, frsem, owner, half)
            if before is not None and step < 2:
                ready += [(owner, core, half) for core in range(N_C) for owner, half in halves]
                continue
            if before is not None and step == 2:
                before()
            run(2 * len(halves) + (4 if 2 <= step < 8 and before is not None else 0))
            ready += [(owner, core, half) for core in range(N_C) for owner, half in halves]
        run(len(ready))

    for half, starts in ((1, (0, 4, 5)), (0, (1, 2, 3))):
        for k in starts:
            move(hid, hs, hr, k)
        forward(hid, hfs, hfr, (0, 0), half)
    kvacc[...] = jnp.zeros_like(kvacc)
    qacc[...] = jnp.zeros_like(qacc)

    def lanes_of(j):
        return pl.ds(pl.multiple_of(j * SHARD, SHARD), SHARD)

    def clip(j, half):
        lanes = lanes_of(j)
        thresh = base_ref[:, lanes] * (1.0 + pct_ref[:, lanes].astype(f32) / 32.0)
        over = gain_ref[:, lanes] / thresh
        step = step_ref[:, lanes]

        rows = pl.ds(half * 128, 128)
        near = pl.ds(half * 256, 128)
        rest = pl.ds(half * 256 + 128, 128)
        x = hid[j, rows, :].astype(f32)
        scale = rs[rows, :]
        for l in range(SHARD // 128):
            cut = slice(l * 128, l * 128 + 128)
            ratio = x[:, cut] * scale * over[:, cut]
            bent = jnp.tanh(ratio)
            xs[j, near, cut] = (thresh[:, cut] * bent).astype(bf16)
            slope = bent - ratio * (1.0 - bent * bent)
            slopes[j, rows, cut] = slope
            xs[j, rest, cut] = (slope * step[:, cut]).astype(bf16)

    late = []

    def query(j):
        qacc[...] += jnp.dot(xs[j], wq[lanes_of(j), :], preferred_element_type=f32)

    def project(j):
        kvacc[...] += nt(xs[j], wkv[:, lanes_of(j)])
        late.append(j)
        if len(late) > LATE:
            query(late.pop(0))


    def norms():
        for rel in PEERS:
            i = ridx(rel)
            arrived(ssr.at[source(me, rel)], sss.at[i], ssrs.at[i])
        total = jnp.sum(ssr[...], axis=0)
        scale = lax.rsqrt(total / WIDTH + EPSILON)
        rs[...] = jnp.transpose(jnp.broadcast_to(scale[0:1, :], (128, TOK)))

        for load in loads[:3]:
            load.wait()

    gather(hid, hs, hr, hfs, hfr, clip, project, norms)

    kvt[...] = nt(permutation(), kvacc[...].astype(bf16)).astype(bf16)

    def block(chip):
        return pl.ds(pl.multiple_of(chip * 16, 16), 16)

    kvr[me] = kvt[block(me // N_C), :]
    for rel in PEERS:
        i = ridx(rel)
        to = peer(me, rel)
        send(kvt.at[block(to // N_C)], kvr.at[me], kvs.at[i], kvrs.at[i], to)

    for j in late:
        query(j)
    for h in range(HEADS):
        cut = slice(h * 128, h * 128 + 128)
        for half in range(2):
            rows = pl.ds(half * 128, 128)
            for out, top in ((qp, 0), (qt, 128)):
                z = qacc[pl.ds(half * 256 + top, 128), cut]
                out[rows, cut] = (z * cos_ref[rows, :] + pltpu.roll(z, 64, 1) * sin_ref[rows, :]).astype(bf16)

    for rel in PEERS:
        i = ridx(rel)
        arrived(kvr.at[source(me, rel)], kvs.at[i], kvrs.at[i])
    both = kvr[...].astype(f32)
    keys = both[:, 0:8, :].reshape(HEAD_DIM, 2 * TOK)
    vals = both[:, 8:16, :].reshape(HEAD_DIM, 2 * TOK).astype(bf16)
    for half in range(2):
        vp[:, half * 128 : half * 128 + 128] = vals[:, half * 256 : half * 256 + 128]
        vt[:, half * 128 : half * 128 + 128] = vals[:, half * 256 + 128 : half * 256 + 256]
    cost, sint = cost_ref[...], sint_ref[...]
    for out, left in ((kp, 0), (kt, 128)):
        z = jnp.concatenate([keys[:, left : left + 128], keys[:, left + 256 : left + 384]], axis=1)
        front, back = z[:64], z[64:]
        out[0:64, :] = (front * cost - back * sint).astype(bf16)
        out[64:128, :] = (back * cost + front * sint).astype(bf16)

    same = jnp.concatenate([docs[...], docs[...]], axis=1) == doc_ref[...].astype(f32)
    place = lax.broadcasted_iota(jnp.int32, (TOK, TOK), 0) >= lax.broadcasted_iota(jnp.int32, (TOK, TOK), 1)
    allowed = same & place
    score_scale = HEAD_DIM ** (-0.5)

    def dot(a, b):
        return jnp.dot(a, b, preferred_element_type=f32)

    for h in range(HEADS):
        cut = slice(h * 128, h * 128 + 128)
        q0, q1 = qp[:, cut], qt[:, cut]
        scores = jnp.where(allowed, dot(q0, kp[...]) * score_scale, MASKED)
        grown = jnp.exp(scores - jnp.max(scores, axis=1, keepdims=True))
        prob = grown / jnp.sum(grown, axis=1, keepdims=True)
        probs[h] = prob
        t = (dot(q1, kp[...]) + dot(q0, kt[...])) * score_scale
        tan = (prob * (t - jnp.sum(prob * t, axis=1, keepdims=True))).astype(bf16)
        ctx[:, cut] = (nt(tan, vp[...]) + nt(prob.astype(bf16), vt[...])).astype(bf16)

    loads[3].wait()

    def slot(chip):
        return chip[0] * N_Z + chip[1]

    def pair_part(s):
        i = slot(PARTS[s])
        pair_out[i] = dot(ctx[...], wo[:, lanes_of(peer(me, PARTS[s] + (1,)))]).astype(bf16)
        send(pair_out.at[i], pair_in.at[i], ps.at[i], pr.at[i], sibling)

    def give(k):
        chip, rows, way = SUMS[k]
        start, size = ROWS[rows]
        send(part.at[slot(chip), pl.ds(start, size)], sums.at[k, pl.ds(0, size)], qs.at[k], qr.at[k], peer(me, way + (0,)))

    def own_part(s):
        i = slot(PARTS[s])
        mine = dot(ctx[...], wo[:, lanes_of(peer(me, PARTS[s] + (0,)))]).astype(bf16).astype(f32)
        arrived(pair_in.at[i], ps.at[i], pr.at[i])
        part[i] = (mine + pair_in[i].astype(f32)).astype(bf16)
        for k in FIRST.get(PARTS[s], ()):
            give(k)

    def add(rows, into, *parts):
        chip, out = into
        start, size = ROWS[rows]
        for k in parts:
            arrived(sums.at[k, pl.ds(0, ROWS[SUMS[k][1]][1])], qs.at[k], qr.at[k])
        value = part[slot(chip), pl.ds(start, size), :].astype(f32)
        for k in parts:
            low = start - ROWS[SUMS[k][1]][0]
            value = value + sums[k, pl.ds(low, size), :].astype(f32)
        if out is None:
            part[slot(chip), pl.ds(start, size), :] = value.astype(bf16)
        else:
            out[me, pl.ds(start, size), :] = value.astype(bf16)

    def take(rows, chip, *parts):
        add(rows, (chip, None), *parts)

    pair_part(0)
    pair_part(1)
    for s in range(8):
        if s + 2 < 8:
            pair_part(s + 2)
        own_part(s)
        if s == 5:
            take("2", (1, 3), 3)
            give(10)
            take("3", (1, 1), 4)
            give(9)
    take("A", (0, 2), 0)
    give(5)
    give(6)
    take("2", (0, 3), 7)
    give(16)
    take("3", (0, 1), 8)
    give(15)
    take("B", (1, 0), 9, 10)
    give(12)
    take("1", (0, 1), 6)
    take("A", (0, 1), 1)
    give(13)
    take("0", (0, 3), 5)
    take("A", (0, 3), 2)
    give(14)
    add("B", ((0, 0), tg), 12, 15, 16)
    for k in (0, 4, 5):
        move(tg, gs, gr, k)
    forward(tg, gfs, gfr, (0, 0), 1)
    add("A", ((0, 0), tg), 11, 13, 14)
    for k in (1, 2, 3):
        move(tg, gs, gr, k)
    forward(tg, gfs, gfr, (0, 0), 0)
    result = pltpu.make_async_copy(tg.at[me], out_hbm, wsem.at[0])
    result.start()
    bacc[...] = jnp.zeros_like(bacc)

    def back(j):
        bacc[...] += nt(tg[j], wo[:, lanes_of(j)])

    gather(tg, gs, gr, gfs, gfr, lambda j, half: None, back, None)

    gk = jnp.zeros((HEAD_DIM, TOK), f32)
    gv = jnp.zeros((HEAD_DIM, TOK), f32)
    marks = []
    for h in range(HEADS):
        cut = slice(h * 128, h * 128 + 128)
        bc = bacc[:, cut].astype(bf16)
        prob = probs[h]
        g = dot(bc, vp[...])
        score = (prob * (g - jnp.sum(prob * g, axis=1, keepdims=True)) * score_scale).astype(bf16)
        marks.append(score)
        gk = gk + tn(qp[:, cut], score)
        gv = gv + tn(bc, prob.astype(bf16))
    front, back_half = gk[:64], gk[64:]
    gk = jnp.concatenate([front * cost + back_half * sint, back_half * cost - front * sint], axis=0)
    gkv_out[...] = jnp.concatenate([gk.reshape(N_T, 8, TOK), gv.reshape(N_T, 8, TOK)], axis=1).astype(bf16)
    for rel in PEERS[::-1]:
        i = ridx(rel)
        to = peer(me, rel)
        send(gkv_out.at[to], gkv_in.at[me], ks.at[i], kr.at[i], to)
    gkv_in[me] = gkv_out[me]
    for h in range(HEADS):
        cut = slice(h * 128, h * 128 + 128)
        z = nt(marks[h], kp[...])
        gq[:, cut] = (z * cos_ref[...] - pltpu.roll(z, 64, 1) * sin_ref[...]).astype(bf16)

    def column_sums(product):
        line = jnp.sum(product, axis=0, keepdims=True)
        return jnp.concatenate([line[:, l * 128 : l * 128 + 128] for l in range(4)] * 2, axis=0)

    def query_step(j, carry):
        gnv[j] = column_sums(nt(gq[...], wq[lanes_of(j), :]) * slopes[j])
        return carry

    lax.fori_loop(0, N_T, query_step, 0, unroll=4)
    for rel in PEERS:
        i = ridx(rel)
        arrived(gkv_in.at[source(me, rel)], ks.at[i], kr.at[i])
    pairs = gkv_in[...].astype(f32).reshape(N_T // 2, 2, 16, TOK)
    summed = (pairs[:, 0] + pairs[:, 1]).reshape(HEAD_DIM, TOK).astype(bf16)
    gkv[...] = tn(summed, permutation()).astype(bf16)

    def key_step(j, carry):
        gnv[j] += column_sums(dot(gkv[...], wkv[:, lanes_of(j)]) * slopes[j])
        return carry

    lax.fori_loop(0, N_T, key_step, 0, unroll=4)
    gnv_in[me] = gnv[me]
    for rel in PEERS:
        i = ridx(rel)
        to = peer(me, rel)
        send(gnv.at[to], gnv_in.at[me], ns.at[i], nr.at[i], to)
    for rel in PEERS:
        i = ridx(rel)
        arrived(gnv_in.at[source(me, rel)], ns.at[i], nr.at[i])
    dpv[...] = jnp.sum(gnv_in[...], axis=0)
    dpv_in[dp] = dpv[...]
    for d in range(1, N_DP):
        send(dpv, dpv_in.at[dp], ds.at[d], dr.at[d], me, (dp + d) % N_DP)
    for d in range(1, N_DP):
        arrived(dpv_in.at[(dp + N_DP - d) % N_DP], ds.at[d], dr.at[d])
    gn_ref[...] = jnp.sum(dpv_in[...], axis=0)[0:4, :]
    result.wait()
    for cp in sends:
        cp.wait_send()


VM = pl.BlockSpec(memory_space=pltpu.VMEM)
ANY = pl.BlockSpec(memory_space=pl.ANY)


def whole(*operands):
    sds = jax.ShapeDtypeStruct
    sem = pltpu.SemaphoreType.DMA((18,))
    vm = pltpu.VMEM
    return pl.pallas_call(
        body,
        name="block",
        out_shape=[sds((TOK, SHARD), bf16), sds((4, 128), f32)],
        in_specs=[ANY] * 14,
        out_specs=[ANY, VM],
        scratch_shapes=[
            vm((1, WIDTH), f32),
            vm((1, WIDTH), f32),
            vm((1, WIDTH), jnp.int32),
            vm((1, WIDTH), f32),
            vm((1, TOK), jnp.int32),
            vm((TOK, 128), f32),
            vm((TOK, 128), f32),
            vm((64, TOK), f32),
            vm((64, TOK), f32),
            vm((N_T, TOK, SHARD), bf16),
            vm((N_T, 2 * TOK, SHARD), bf16),
            vm((N_T, TOK, SHARD), f32),
            vm((WIDTH, SHARD), bf16),
            vm((128, WIDTH), bf16),
            vm((SHARD, WIDTH), bf16),
            vm((8, TOK), f32),
            vm((N_T, 8, TOK), f32),
            vm((TOK, 128), f32),
            vm((2 * TOK, 128), f32),
            vm((2 * TOK, SHARD), f32),
            vm((128, 2 * TOK), bf16),
            vm((N_T, 16, 2 * TOK), bf16),
            vm((TOK, SHARD), bf16),
            vm((TOK, SHARD), bf16),
            vm((HEAD_DIM, TOK), bf16),
            vm((HEAD_DIM, TOK), bf16),
            vm((HEAD_DIM, TOK), bf16),
            vm((HEAD_DIM, TOK), bf16),
            vm((TOK, 128), f32),
            vm((HEADS, TOK, TOK), f32),
            vm((TOK, SHARD), bf16),
            vm((8, TOK, SHARD), bf16),
            vm((8, TOK, SHARD), bf16),
            vm((8, TOK, SHARD), bf16),
            vm((len(SUMS), 128, SHARD), bf16),
            vm((N_T, TOK, SHARD), bf16),
            vm((TOK, SHARD), f32),
            vm((TOK, SHARD), bf16),
            vm((N_T, 16, TOK), bf16),
            vm((N_T, 16, TOK), bf16),
            vm((TOK, 128), bf16),
            vm((N_T, 8, 128), f32),
            vm((N_T, 8, 128), f32),
            vm((8, 128), f32),
            vm((N_DP, 8, 128), f32),
            pltpu.SemaphoreType.DMA((14,)),
        ]
        + [sem] * 22,
        compiler_params=pltpu.CompilerParams(collective_id=1, has_side_effects=True, vmem_limit_bytes=VMEM_BYTES),
    )(*operands)


def finish_body(shard_ref, gn_ref, out_ref, mean_ref):
    out_ref[...] = shard_ref[...]
    mean_ref[...] = gn_ref[...] / (TOK * N_DP)


def finish(shard, gn):
    sds = jax.ShapeDtypeStruct
    return pl.pallas_call(
        finish_body,
        name="finish",
        out_shape=[sds((TOK, SHARD), bf16), sds((4, 128), f32)],
        in_specs=[VM] * 2,
        out_specs=[VM] * 2,
    )(shard, gn)


def tables():
    positions = np.arange(TOK, dtype=np.float32)
    frequency = np.exp(np.float32(-math.log(ROPE_BASE) * 2.0) * np.arange(64, dtype=np.float32) / np.float32(HEAD_DIM))
    angles = positions[:, None] * frequency[None, :].astype(np.float32)
    cosine, sine = np.cos(angles), np.sin(angles)
    return (
        np.concatenate([cosine, cosine], axis=1),
        np.concatenate([-sine, sine], axis=1),
        np.ascontiguousarray(cosine.T),
        np.ascontiguousarray(sine.T),
    )


def on_device(
    hidden_in, norm_gain, clip_base, pct_index, clip_step, w_query, w_key, w_value, w_out, doc_ids
):
    row = lambda v: v.reshape(1, WIDTH)
    tangent_shard, gn = whole(
        hidden_in, row(norm_gain), row(clip_base), row(pct_index), row(clip_step), doc_ids,
        *(jnp.asarray(t) for t in tables()),
        w_query, w_key.T, w_value.T, w_out,
    )
    tangent_shard, gn = finish(tangent_shard, gn)
    return (tangent_shard, gn.reshape(SHARD))


def solution(mesh):
    in_specs = (
        P("dp", "tensor"),
        P(),
        P(),
        P(),
        P(),
        P(None, "tensor"),
        P(None, "tensor"),
        P(None, "tensor"),
        P("tensor", None),
        P("dp", None),
    )
    out_specs = (P("dp", "tensor"), P("tensor"))
    return jax.shard_map(
        on_device, mesh=mesh, in_specs=in_specs, out_specs=out_specs, check_vma=False
    )
```

```python
import functools
import math

import jax
import jax.numpy as jnp
import numpy as np
from jax import lax
from jax.experimental import pallas as pl
from jax.experimental.pallas import tpu as pltpu
from jax.sharding import PartitionSpec as P

HEAD_DIM = 128
EPSILON = 1e-05
ROPE_BASE = 500000.0
MASKED = -1e30
MESH = pl.DeviceIdType.MESH
f32 = jnp.float32
bf16 = jnp.bfloat16

N_Y, N_Z, N_C = 2, 4, 2
N_T = N_Y * N_Z * N_C
TOK = 256
SHARD = 512
WIDTH = N_T * SHARD
HEADS = 4
N_DP = 8
VMEM_BYTES = 60 << 20

RELS = [(dy, dz, dc) for dy in range(N_Y) for dz in range(N_Z) for dc in range(N_C)]
PEERS = [r for r in RELS if r != (0, 0, 0)]
ROWS = {"A": (0, 112), "B": (112, 144), "0": (0, 48), "1": (48, 64), "2": (112, 80), "3": (192, 64)}
Y, ZP, ZM = (1, 0), (0, 1), (0, 3)

MOVES = [
    ((0, 0), "B", Y), ((0, 0), "A", Y), ((0, 0), "A", ZP), ((0, 0), "A", ZM), ((0, 0), "B", ZP), ((0, 0), "B", ZM),
    ((0, 3), "0", ZP), ((0, 1), "1", ZM), ((0, 3), "2", ZP), ((0, 1), "3", ZM), ((0, 3), "A", Y), ((0, 1), "A", Y),
    ((1, 0), "B", ZP), ((1, 0), "B", ZM), ((1, 3), "2", ZP), ((1, 1), "3", ZM), ((0, 2), "0", Y), ((0, 2), "1", Y),
]
EVENTS = [
    ([0], [12, 13], [((1, 0), 1)]),
    ([2], [10, 6], [((0, 3), 0)]),
    ([3], [11, 7], [((0, 1), 0)]),
    ([1], [], [((1, 0), 0)]),
    ([4], [8], [((0, 3), 1)]),
    ([5], [9], [((0, 1), 1)]),
    ([6, 7], [16, 17], [((0, 2), 0)]),
    ([12, 13], [14, 15], [((1, 3), 1), ((1, 1), 1)]),
    ([8, 9], [], [((0, 2), 1)]),
    ([10, 11], [], [((1, 3), 0), ((1, 1), 0)]),
    ([14, 15], [], [((1, 2), 1)]),
    ([16, 17], [], [((1, 2), 0)]),
]
SUMS = [
    ((1, 2), "A", Y), ((1, 1), "A", Y), ((1, 3), "A", Y), ((1, 2), "2", ZM), ((1, 2), "3", ZP),
    ((0, 2), "0", ZM), ((0, 2), "1", ZP), ((0, 2), "2", ZM), ((0, 2), "3", ZP), ((1, 1), "B", ZP), ((1, 3), "B", ZM),
    ((1, 0), "A", Y), ((1, 0), "B", Y), ((0, 1), "A", ZP), ((0, 3), "A", ZM), ((0, 1), "B", ZP), ((0, 3), "B", ZM),
]
PARTS = [(1, 2), (1, 1), (1, 3), (0, 2), (1, 0), (0, 1), (0, 3), (0, 0)]
FIRST = {(1, 2): [0, 3, 4], (1, 1): [1], (1, 3): [2], (0, 2): [7, 8], (1, 0): [11]}

FAR = [chip + (core,) for chip in PARTS for core in (1, 0)][:-1]


def minus(a, b):
    return ((a[0] - b[0]) % N_Y, (a[1] - b[1]) % N_Z)


def ridx(rel):
    return (rel[0] * N_Z + rel[1]) * N_C + rel[2]


def peer(me, rel):
    y, z, c = me // (N_Z * N_C), (me // N_C) % N_Z, me % N_C
    y = (y + rel[0]) % N_Y
    z = (z + rel[1]) % N_Z
    c = (c + rel[2]) % N_C
    return (y * N_Z + z) * N_C + c


def source(me, rel):
    return peer(me, (-rel[0], -rel[1], -rel[2]))


def remote(src, dst, ssem, rsem, dp, target):
    return pltpu.make_async_remote_copy(
        src_ref=src, dst_ref=dst, send_sem=ssem, recv_sem=rsem, device_id=(dp, target), device_id_type=MESH
    )


def nt(a, b):
    return lax.dot_general(a, b, (((1,), (1,)), ((), ())), preferred_element_type=f32)


def tn(a, b):
    return lax.dot_general(a, b, (((0,), (0,)), ((), ())), preferred_element_type=f32)


def permutation():
    row = lax.broadcasted_iota(jnp.int32, (128, 128), 0)
    col = lax.broadcasted_iota(jnp.int32, (128, 128), 1)
    head, low = row // 16, row % 16
    want = jnp.where(low < 8, low * 8 + head, 64 + (low - 8) * 8 + head)
    return (col == want).astype(f32).astype(bf16)


def body(
    x_hbm, gain_hbm, base_hbm, pct_hbm, step_hbm, doc_hbm, cos_hbm, sin_hbm, cost_hbm, sint_hbm,
    wq_hbm, wk_hbm, wv_hbm, wo_hbm,
    out_hbm, gn_ref,
    gain_ref, base_ref, pct_ref, step_ref, doc_ref, cos_ref, sin_ref, cost_ref, sint_ref,
    hid, xs, slopes, wq, wkv, wo, ss_send, ssr, rs, kvacc, qacc, kvt, kvr, qp, qt, kp, kt, vp, vt, docs, probs, ctx,
    pair_out, pair_in, part, sums, tg, bacc, gq, gkv_out, gkv_in, gkv, gnv, gnv_in, dpv, dpv_in,
    wsem, hs, hr, hfs, hfr, sss, ssrs, kvs, kvrs, ps, pr, qs, qr, gs, gr, gfs, gfr, ks, kr, ns, nr, ds, dr,
):
    me = lax.axis_index("tensor")
    dp = lax.axis_index("dp")
    sibling = peer(me, (0, 0, 1))
    barrier = pltpu.get_barrier_semaphore()
    for rel in PEERS:
        pl.semaphore_signal(barrier, inc=1, device_id=(dp, peer(me, rel)), device_id_type=MESH)
    for d in range(1, N_DP):
        pl.semaphore_signal(barrier, inc=1, device_id=((dp + d) % N_DP, me), device_id_type=MESH)
    copies = [
        (x_hbm, hid.at[me]), (doc_hbm, doc_ref), (gain_hbm, gain_ref), (base_hbm, base_ref), (pct_hbm, pct_ref),
        (step_hbm, step_ref), (cos_hbm, cos_ref), (sin_hbm, sin_ref), (cost_hbm, cost_ref), (sint_hbm, sint_ref),
    ]
    small = [pltpu.make_async_copy(a, b, wsem.at[4 + i]) for i, (a, b) in enumerate(copies)]
    for load in small:
        load.start()
    loads = [
        pltpu.make_async_copy(wk_hbm, wkv.at[pl.ds(0, 64)], wsem.at[0]),
        pltpu.make_async_copy(wv_hbm, wkv.at[pl.ds(64, 64)], wsem.at[1]),
        pltpu.make_async_copy(wq_hbm, wq, wsem.at[2]),
        pltpu.make_async_copy(wo_hbm, wo, wsem.at[3]),
    ]
    for load in loads:
        load.start()

    sends = []

    def send(src, dst, ssem, rsem, to, group=None):
        cp = remote(src, dst, ssem, rsem, dp if group is None else group, to)
        cp.start()
        sends.append(cp)

    def arrived(dst, ssem, rsem):
        remote(dst, dst, ssem, rsem, dp, me).wait_recv()

    small[0].wait()
    own = hid[me].astype(f32)
    square = own * own
    high = square.astype(bf16)
    low = (square - high.astype(f32)).astype(bf16)
    ones = jnp.ones((8, SHARD), bf16)
    ss_send[...] = nt(ones, high) + nt(ones, low)
    ssr[me] = ss_send[...]
    for load in small[1:]:
        load.wait()
    docs[...] = jnp.transpose(jnp.broadcast_to(doc_ref[...].astype(f32), (128, TOK)))

    pl.semaphore_wait(barrier, len(PEERS) + N_DP - 1)
    for rel in FAR:
        i = ridx(rel)
        send(ss_send, ssr.at[me], sss.at[i], ssrs.at[i], peer(me, rel))

    def piece(buf, owner, rows):
        start, size = ROWS[rows]
        return buf.at[peer(me, owner + (0,)), pl.ds(start, size)]

    def move(buf, ssem, rsem, k):
        owner, rows, way = MOVES[k]
        ref = piece(buf, owner, rows)
        send(ref, ref, ssem.at[k], rsem.at[k], peer(me, way + (0,)))

    def moved(buf, ssem, rsem, k):
        owner, rows, way = MOVES[k]
        arrived(piece(buf, minus(owner, way), rows), ssem.at[k], rsem.at[k])

    def forward(buf, ssem, rsem, owner, half):
        i = (owner[0] * N_Z + owner[1]) * 2 + half
        ref = piece(buf, owner, "AB"[half])
        send(ref, ref, ssem.at[i], rsem.at[i], sibling)

    def gather(buf, ssem, rsem, fssem, frsem, use_half, use_block, before):
        ready = [((0, 0), c, h) for c in range(N_C) for h in range(2)]
        done = set()

        def run(count):
            for owner, core, half in ready[:count]:
                j = peer(me, owner + (core,))
                if core == 1:
                    i = (owner[0] * N_Z + owner[1]) * 2 + half
                    arrived(buf.at[j, pl.ds(*ROWS["AB"[half]])], fssem.at[i], frsem.at[i])
                use_half(j, half)
                done.add((owner, core, half))
                if (owner, core, 1 - half) in done:
                    use_block(j)
            del ready[:count]

        for step, (waits, starts, halves) in enumerate(EVENTS):
            for k in waits:
                moved(buf, ssem, rsem, k)
            for k in starts:
                move(buf, ssem, rsem, k)
            for owner, half in halves:
                forward(buf, fssem, frsem, owner, half)
            if before is not None and step < 2:
                ready += [(owner, core, half) for core in range(N_C) for owner, half in halves]
                continue
            if before is not None and step == 2:
                before()
            run(2 * len(halves) + (4 if 2 <= step < 8 and before is not None else 0))
            ready += [(owner, core, half) for core in range(N_C) for owner, half in halves]
        run(len(ready))

    for k in (0, 2, 3, 1, 4, 5):
        move(hid, hs, hr, k)
    for half in range(2):
        forward(hid, hfs, hfr, (0, 0), half)
    kvacc[...] = jnp.zeros_like(kvacc)
    qacc[...] = jnp.zeros_like(qacc)

    def lanes_of(j):
        return pl.ds(pl.multiple_of(j * SHARD, SHARD), SHARD)

    def clip(j, half):
        lanes = lanes_of(j)
        thresh = base_ref[:, lanes] * (1.0 + pct_ref[:, lanes].astype(f32) / 32.0)
        over = gain_ref[:, lanes] / thresh
        step = step_ref[:, lanes]

        start, size = ROWS["AB"[half]]
        rows = pl.ds(start, size)
        rest = pl.ds(TOK + start, size)
        x = hid[j, rows, :].astype(f32)
        scale = rs[rows, :]
        for l in range(SHARD // 128):
            cut = slice(l * 128, l * 128 + 128)
            ratio = x[:, cut] * scale * over[:, cut]
            bent = jnp.tanh(ratio)
            xs[j, rows, cut] = (thresh[:, cut] * bent).astype(bf16)
            slope = bent - ratio * (1.0 - bent * bent)
            slopes[j, rows, cut] = slope
            xs[j, rest, cut] = (slope * step[:, cut]).astype(bf16)

    def project(j):
        kvacc[...] += nt(xs[j], wkv[:, lanes_of(j)])


    def norms():
        for rel in PEERS:
            i = ridx(rel)
            arrived(ssr.at[source(me, rel)], sss.at[i], ssrs.at[i])
        total = jnp.sum(ssr[...], axis=0)
        scale = lax.rsqrt(total / WIDTH + EPSILON)
        rs[...] = jnp.transpose(jnp.broadcast_to(scale[0:1, :], (128, TOK)))

        for load in loads[:2]:
            load.wait()

    gather(hid, hs, hr, hfs, hfr, clip, project, norms)

    kvt[...] = nt(permutation(), kvacc[...].astype(bf16)).astype(bf16)

    def block(chip):
        return pl.ds(pl.multiple_of(chip * 16, 16), 16)

    kvr[me] = kvt[block(me // N_C), :]
    for rel in FAR:
        i = ridx(rel)
        to = peer(me, rel)
        send(kvt.at[block(to // N_C)], kvr.at[me], kvs.at[i], kvrs.at[i], to)

    def query_four(r, carry):
        value = qacc[...]
        for i in range(4):
            j = r * 4 + i
            value = value + jnp.dot(xs[j], wq[lanes_of(j), :], preferred_element_type=f32)
        qacc[...] = value
        return carry

    loads[2].wait()
    lax.fori_loop(0, N_T // 4, query_four, 0)
    for h in range(HEADS):
        cut = slice(h * 128, h * 128 + 128)
        for out, top in ((qp, 0), (qt, TOK)):
            z = qacc[pl.ds(top, TOK), cut]
            out[:, cut] = (z * cos_ref[...] + pltpu.roll(z, 64, 1) * sin_ref[...]).astype(bf16)

    for rel in PEERS:
        i = ridx(rel)
        arrived(kvr.at[source(me, rel)], kvs.at[i], kvrs.at[i])
    both = kvr[...].astype(f32)
    keys = both[:, 0:8, :].reshape(HEAD_DIM, 2 * TOK)
    vals = both[:, 8:16, :].reshape(HEAD_DIM, 2 * TOK).astype(bf16)
    vp[...] = vals[:, :TOK]
    vt[...] = vals[:, TOK:]
    cost, sint = cost_ref[...], sint_ref[...]
    for out, left in ((kp, 0), (kt, TOK)):
        z = keys[:, left : left + TOK]
        front, back = z[:64], z[64:]
        out[0:64, :] = (front * cost - back * sint).astype(bf16)
        out[64:128, :] = (back * cost + front * sint).astype(bf16)

    same = jnp.concatenate([docs[...], docs[...]], axis=1) == doc_ref[...].astype(f32)
    place = lax.broadcasted_iota(jnp.int32, (TOK, TOK), 0) >= lax.broadcasted_iota(jnp.int32, (TOK, TOK), 1)
    allowed = same & place
    score_scale = HEAD_DIM ** (-0.5)

    def dot(a, b):
        return jnp.dot(a, b, preferred_element_type=f32)

    for h in range(HEADS):
        cut = slice(h * 128, h * 128 + 128)
        q0, q1 = qp[:, cut], qt[:, cut]
        scores = jnp.where(allowed, dot(q0, kp[...]) * score_scale, MASKED)
        grown = jnp.exp(scores - jnp.max(scores, axis=1, keepdims=True))
        prob = grown / jnp.sum(grown, axis=1, keepdims=True)
        probs[h] = prob
        t = (dot(q1, kp[...]) + dot(q0, kt[...])) * score_scale
        tan = (prob * (t - jnp.sum(prob * t, axis=1, keepdims=True))).astype(bf16)
        ctx[:, cut] = (nt(tan, vp[...]) + nt(prob.astype(bf16), vt[...])).astype(bf16)

    loads[3].wait()

    def slot(chip):
        return chip[0] * N_Z + chip[1]

    def pair_part(s):
        i = slot(PARTS[s])
        pair_out[i] = dot(ctx[...], wo[:, lanes_of(peer(me, PARTS[s] + (1,)))]).astype(bf16)
        send(pair_out.at[i], pair_in.at[i], ps.at[i], pr.at[i], sibling)

    def give(k):
        chip, rows, way = SUMS[k]
        start, size = ROWS[rows]
        send(part.at[slot(chip), pl.ds(start, size)], sums.at[k, pl.ds(0, size)], qs.at[k], qr.at[k], peer(me, way + (0,)))

    def own_part(s):
        i = slot(PARTS[s])
        mine = dot(ctx[...], wo[:, lanes_of(peer(me, PARTS[s] + (0,)))]).astype(bf16).astype(f32)
        arrived(pair_in.at[i], ps.at[i], pr.at[i])
        part[i] = (mine + pair_in[i].astype(f32)).astype(bf16)
        for k in FIRST.get(PARTS[s], ()):
            give(k)

    def add(rows, into, *parts):
        chip, out = into
        start, size = ROWS[rows]
        for k in parts:
            arrived(sums.at[k, pl.ds(0, ROWS[SUMS[k][1]][1])], qs.at[k], qr.at[k])
        value = part[slot(chip), pl.ds(start, size), :].astype(f32)
        for k in parts:
            low = start - ROWS[SUMS[k][1]][0]
            value = value + sums[k, pl.ds(low, size), :].astype(f32)
        if out is None:
            part[slot(chip), pl.ds(start, size), :] = value.astype(bf16)
        else:
            out[me, pl.ds(start, size), :] = value.astype(bf16)

    def take(rows, chip, *parts):
        add(rows, (chip, None), *parts)

    pair_part(0)
    pair_part(1)
    for s in range(8):
        if s + 2 < 8:
            pair_part(s + 2)
        own_part(s)
        if s == 5:
            take("2", (1, 3), 3)
            give(10)
            take("3", (1, 1), 4)
            give(9)
    take("A", (0, 2), 0)
    give(5)
    give(6)
    take("2", (0, 3), 7)
    give(16)
    take("3", (0, 1), 8)
    give(15)
    take("B", (1, 0), 9, 10)
    give(12)
    take("1", (0, 1), 6)
    take("A", (0, 1), 1)
    give(13)
    take("0", (0, 3), 5)
    take("A", (0, 3), 2)
    give(14)
    add("B", ((0, 0), tg), 12, 15, 16)
    move(tg, gs, gr, 0)
    add("A", ((0, 0), tg), 11, 13, 14)
    for k in (2, 3, 1, 4, 5):
        move(tg, gs, gr, k)
    for half in range(2):
        forward(tg, gfs, gfr, (0, 0), half)
    result = pltpu.make_async_copy(tg.at[me], out_hbm, wsem.at[0])
    result.start()
    bacc[...] = jnp.zeros_like(bacc)

    def back(j):
        bacc[...] += nt(tg[j], wo[:, lanes_of(j)])

    gather(tg, gs, gr, gfs, gfr, lambda j, half: None, back, None)

    gk = jnp.zeros((HEAD_DIM, TOK), f32)
    gv = jnp.zeros((HEAD_DIM, TOK), f32)
    marks = []
    for h in range(HEADS):
        cut = slice(h * 128, h * 128 + 128)
        bc = bacc[:, cut].astype(bf16)
        prob = probs[h]
        g = dot(bc, vp[...])
        score = (prob * (g - jnp.sum(prob * g, axis=1, keepdims=True)) * score_scale).astype(bf16)
        marks.append(score)
        gk = gk + tn(qp[:, cut], score)
        gv = gv + tn(bc, prob.astype(bf16))
    front, back_half = gk[:64], gk[64:]
    gk = jnp.concatenate([front * cost + back_half * sint, back_half * cost - front * sint], axis=0)
    gkv_out[...] = jnp.concatenate([gk.reshape(N_T, 8, TOK), gv.reshape(N_T, 8, TOK)], axis=1).astype(bf16)
    for rel in FAR:
        i = ridx(rel)
        to = peer(me, rel)
        send(gkv_out.at[to], gkv_in.at[me], ks.at[i], kr.at[i], to)
    gkv_in[me] = gkv_out[me]
    for h in range(HEADS):
        cut = slice(h * 128, h * 128 + 128)
        z = nt(marks[h], kp[...])
        gq[:, cut] = (z * cos_ref[...] - pltpu.roll(z, 64, 1) * sin_ref[...]).astype(bf16)

    def column_sums(product):
        line = jnp.sum(product, axis=0, keepdims=True)
        return jnp.concatenate([line[:, l * 128 : l * 128 + 128] for l in range(4)] * 2, axis=0)

    def query_step(j, carry):
        gnv[j] = column_sums(nt(gq[...], wq[lanes_of(j), :]) * slopes[j])
        return carry

    lax.fori_loop(0, N_T, query_step, 0, unroll=4)
    for rel in PEERS:
        i = ridx(rel)
        arrived(gkv_in.at[source(me, rel)], ks.at[i], kr.at[i])
    pairs = gkv_in[...].astype(f32).reshape(N_T // 2, 2, 16, TOK)
    summed = (pairs[:, 0] + pairs[:, 1]).reshape(HEAD_DIM, TOK).astype(bf16)
    gkv[...] = tn(summed, permutation()).astype(bf16)

    def key_step(j, carry):
        gnv[j] += column_sums(dot(gkv[...], wkv[:, lanes_of(j)]) * slopes[j])
        return carry

    lax.fori_loop(0, N_T, key_step, 0, unroll=4)
    gnv_in[me] = gnv[me]
    for rel in FAR:
        i = ridx(rel)
        to = peer(me, rel)
        send(gnv.at[to], gnv_in.at[me], ns.at[i], nr.at[i], to)
    for rel in PEERS:
        i = ridx(rel)
        arrived(gnv_in.at[source(me, rel)], ns.at[i], nr.at[i])
    dpv[...] = jnp.sum(gnv_in[...], axis=0)
    dpv_in[dp] = dpv[...]
    for d in (5, 3, 4, 2, 6, 7, 1):
        send(dpv, dpv_in.at[dp], ds.at[d], dr.at[d], me, (dp + d) % N_DP)
    for d in range(1, N_DP):
        arrived(dpv_in.at[(dp + N_DP - d) % N_DP], ds.at[d], dr.at[d])
    gn_ref[...] = jnp.sum(dpv_in[...], axis=0)[0:4, :]
    result.wait()
    for cp in sends:
        cp.wait_send()


VM = pl.BlockSpec(memory_space=pltpu.VMEM)
ANY = pl.BlockSpec(memory_space=pl.ANY)


def whole(*operands):
    sds = jax.ShapeDtypeStruct
    sem = pltpu.SemaphoreType.DMA((18,))
    vm = pltpu.VMEM
    return pl.pallas_call(
        body,
        name="block",
        out_shape=[sds((TOK, SHARD), bf16), sds((4, 128), f32)],
        in_specs=[ANY] * 14,
        out_specs=[ANY, VM],
        scratch_shapes=[
            vm((1, WIDTH), f32),
            vm((1, WIDTH), f32),
            vm((1, WIDTH), jnp.int32),
            vm((1, WIDTH), f32),
            vm((1, TOK), jnp.int32),
            vm((TOK, 128), f32),
            vm((TOK, 128), f32),
            vm((64, TOK), f32),
            vm((64, TOK), f32),
            vm((N_T, TOK, SHARD), bf16),
            vm((N_T, 2 * TOK, SHARD), bf16),
            vm((N_T, TOK, SHARD), f32),
            vm((WIDTH, SHARD), bf16),
            vm((128, WIDTH), bf16),
            vm((SHARD, WIDTH), bf16),
            vm((8, TOK), f32),
            vm((N_T, 8, TOK), f32),
            vm((TOK, 128), f32),
            vm((2 * TOK, 128), f32),
            vm((2 * TOK, SHARD), f32),
            vm((128, 2 * TOK), bf16),
            vm((N_T, 16, 2 * TOK), bf16),
            vm((TOK, SHARD), bf16),
            vm((TOK, SHARD), bf16),
            vm((HEAD_DIM, TOK), bf16),
            vm((HEAD_DIM, TOK), bf16),
            vm((HEAD_DIM, TOK), bf16),
            vm((HEAD_DIM, TOK), bf16),
            vm((TOK, 128), f32),
            vm((HEADS, TOK, TOK), f32),
            vm((TOK, SHARD), bf16),
            vm((8, TOK, SHARD), bf16),
            vm((8, TOK, SHARD), bf16),
            vm((8, TOK, SHARD), bf16),
            vm((len(SUMS), 144, SHARD), bf16),
            vm((N_T, TOK, SHARD), bf16),
            vm((TOK, SHARD), f32),
            vm((TOK, SHARD), bf16),
            vm((N_T, 16, TOK), bf16),
            vm((N_T, 16, TOK), bf16),
            vm((TOK, 128), bf16),
            vm((N_T, 8, 128), f32),
            vm((N_T, 8, 128), f32),
            vm((8, 128), f32),
            vm((N_DP, 8, 128), f32),
            pltpu.SemaphoreType.DMA((14,)),
        ]
        + [sem] * 22,
        compiler_params=pltpu.CompilerParams(collective_id=1, has_side_effects=True, vmem_limit_bytes=VMEM_BYTES),
    )(*operands)


def finish_body(shard_ref, gn_ref, out_ref, mean_ref):
    out_ref[...] = shard_ref[...]
    mean_ref[...] = gn_ref[...] / (TOK * N_DP)


def finish(shard, gn):
    sds = jax.ShapeDtypeStruct
    return pl.pallas_call(
        finish_body,
        name="finish",
        out_shape=[sds((TOK, SHARD), bf16), sds((4, 128), f32)],
        in_specs=[VM] * 2,
        out_specs=[VM] * 2,
    )(shard, gn)


def tables():
    positions = np.arange(TOK, dtype=np.float32)
    frequency = np.exp(np.float32(-math.log(ROPE_BASE) * 2.0) * np.arange(64, dtype=np.float32) / np.float32(HEAD_DIM))
    angles = positions[:, None] * frequency[None, :].astype(np.float32)
    cosine, sine = np.cos(angles), np.sin(angles)
    return (
        np.concatenate([cosine, cosine], axis=1),
        np.concatenate([-sine, sine], axis=1),
        np.ascontiguousarray(cosine.T),
        np.ascontiguousarray(sine.T),
    )


def on_device(
    hidden_in, norm_gain, clip_base, pct_index, clip_step, w_query, w_key, w_value, w_out, doc_ids
):
    row = lambda v: v.reshape(1, WIDTH)
    tangent_shard, gn = whole(
        hidden_in, row(norm_gain), row(clip_base), row(pct_index), row(clip_step), doc_ids,
        *(jnp.asarray(t) for t in tables()),
        w_query, w_key.T, w_value.T, w_out,
    )
    tangent_shard, gn = finish(tangent_shard, gn)
    return (tangent_shard, gn.reshape(SHARD))


def solution(mesh):
    in_specs = (
        P("dp", "tensor"),
        P(),
        P(),
        P(),
        P(),
        P(None, "tensor"),
        P(None, "tensor"),
        P(None, "tensor"),
        P("tensor", None),
        P("dp", None),
    )
    out_specs = (P("dp", "tensor"), P("tensor"))
    return jax.shard_map(
        on_device, mesh=mesh, in_specs=in_specs, out_specs=out_specs, check_vma=False
    )
```

```python
import functools
import math

import jax
import jax.numpy as jnp
import numpy as np
from jax import lax
from jax.experimental import pallas as pl
from jax.experimental.pallas import tpu as pltpu
from jax.sharding import PartitionSpec as P

HEAD_DIM = 128
EPSILON = 1e-05
ROPE_BASE = 500000.0
MASKED = -1e30
MESH = pl.DeviceIdType.MESH
f32 = jnp.float32
bf16 = jnp.bfloat16

N_Y, N_Z, N_C = 2, 4, 2
N_T = N_Y * N_Z * N_C
TOK = 256
SHARD = 512
WIDTH = N_T * SHARD
HEADS = 4
N_DP = 8
VMEM_BYTES = 60 << 20

RELS = [(dy, dz, dc) for dy in range(N_Y) for dz in range(N_Z) for dc in range(N_C)]
PEERS = [r for r in RELS if r != (0, 0, 0)]
ROWS = {"A": (0, 112), "B": (112, 144), "0": (0, 48), "1": (48, 64), "2": (112, 80), "3": (192, 64)}
Y, ZP, ZM = (1, 0), (0, 1), (0, 3)

MOVES = [
    ((0, 0), "B", Y), ((0, 0), "A", Y), ((0, 0), "A", ZP), ((0, 0), "A", ZM), ((0, 0), "B", ZP), ((0, 0), "B", ZM),
    ((0, 3), "0", ZP), ((0, 1), "1", ZM), ((0, 3), "2", ZP), ((0, 1), "3", ZM), ((0, 3), "A", Y), ((0, 1), "A", Y),
    ((1, 0), "B", ZP), ((1, 0), "B", ZM), ((1, 3), "2", ZP), ((1, 1), "3", ZM), ((0, 2), "0", Y), ((0, 2), "1", Y),
]
EVENTS = [
    ([0], [12, 13], [((1, 0), 1)]),
    ([2], [10, 6], [((0, 3), 0)]),
    ([3], [11, 7], [((0, 1), 0)]),
    ([1], [], [((1, 0), 0)]),
    ([4], [8], [((0, 3), 1)]),
    ([5], [9], [((0, 1), 1)]),
    ([6], [16], []),
    ([7], [17], [((0, 2), 0)]),
    ([12], [14], [((1, 3), 1)]),
    ([13], [15], [((1, 1), 1)]),
    ([8, 9], [], [((0, 2), 1)]),
    ([10, 11], [], [((1, 3), 0), ((1, 1), 0)]),
    ([14, 15], [], [((1, 2), 1)]),
    ([16, 17], [], [((1, 2), 0)]),
]
SUMS = [
    ((1, 2), "A", Y), ((1, 1), "A", Y), ((1, 3), "A", Y), ((1, 2), "2", ZM), ((1, 2), "3", ZP),
    ((0, 2), "0", ZM), ((0, 2), "1", ZP), ((0, 2), "2", ZM), ((0, 2), "3", ZP), ((1, 1), "B", ZP), ((1, 3), "B", ZM),
    ((1, 0), "A", Y), ((1, 0), "B", Y), ((0, 1), "A", ZP), ((0, 3), "A", ZM), ((0, 1), "B", ZP), ((0, 3), "B", ZM),
]
PARTS = [(1, 2), (1, 1), (1, 3), (0, 2), (1, 0), (0, 1), (0, 3), (0, 0)]
FIRST = {(1, 2): [0, 3, 4], (1, 1): [1], (1, 3): [2], (0, 2): [7, 8], (1, 0): [11]}

FAR = [chip + (core,) for chip in PARTS for core in (1, 0)][:-1]


def minus(a, b):
    return ((a[0] - b[0]) % N_Y, (a[1] - b[1]) % N_Z)


def ridx(rel):
    return (rel[0] * N_Z + rel[1]) * N_C + rel[2]


def peer(me, rel):
    y, z, c = me // (N_Z * N_C), (me // N_C) % N_Z, me % N_C
    y = (y + rel[0]) % N_Y
    z = (z + rel[1]) % N_Z
    c = (c + rel[2]) % N_C
    return (y * N_Z + z) * N_C + c


def source(me, rel):
    return peer(me, (-rel[0], -rel[1], -rel[2]))


def remote(src, dst, ssem, rsem, dp, target):
    return pltpu.make_async_remote_copy(
        src_ref=src, dst_ref=dst, send_sem=ssem, recv_sem=rsem, device_id=(dp, target), device_id_type=MESH
    )


def nt(a, b):
    return lax.dot_general(a, b, (((1,), (1,)), ((), ())), preferred_element_type=f32)


def tn(a, b):
    return lax.dot_general(a, b, (((0,), (0,)), ((), ())), preferred_element_type=f32)


def permutation():
    row = lax.broadcasted_iota(jnp.int32, (128, 128), 0)
    col = lax.broadcasted_iota(jnp.int32, (128, 128), 1)
    head, low = row // 16, row % 16
    want = jnp.where(low < 8, low * 8 + head, 64 + (low - 8) * 8 + head)
    return (col == want).astype(f32).astype(bf16)


def body(
    x_hbm, gain_hbm, base_hbm, pct_hbm, step_hbm, doc_hbm, cos_hbm, sin_hbm, cost_hbm, sint_hbm,
    wq_hbm, wk_hbm, wv_hbm, wo_hbm,
    out_hbm, gn_ref,
    gain_ref, base_ref, pct_ref, step_ref, doc_ref, cos_ref, sin_ref, cost_ref, sint_ref,
    hid, xs, slopes, wq, wkv, wo, ss_send, ssr, rs, kvacc, qacc, kvt, kvr, qp, qt, kp, kt, vp, vt, docs, probs, ctx,
    pair_out, pair_in, part, sums, tg, bacc, gq, gkv_out, gkv_in, gkv, gnv, gnv_in, dpv, dpv_in,
    wsem, hs, hr, hfs, hfr, sss, ssrs, kvs, kvrs, ps, pr, qs, qr, gs, gr, gfs, gfr, ks, kr, ns, nr, ds, dr,
):
    me = lax.axis_index("tensor")
    dp = lax.axis_index("dp")
    sibling = peer(me, (0, 0, 1))
    barrier = pltpu.get_barrier_semaphore()
    for rel in PEERS:
        pl.semaphore_signal(barrier, inc=1, device_id=(dp, peer(me, rel)), device_id_type=MESH)
    for d in range(1, N_DP):
        pl.semaphore_signal(barrier, inc=1, device_id=((dp + d) % N_DP, me), device_id_type=MESH)
    copies = [
        (x_hbm, hid.at[me]), (doc_hbm, doc_ref), (gain_hbm, gain_ref), (base_hbm, base_ref), (pct_hbm, pct_ref),
        (step_hbm, step_ref), (cos_hbm, cos_ref), (sin_hbm, sin_ref), (cost_hbm, cost_ref), (sint_hbm, sint_ref),
    ]
    small = [pltpu.make_async_copy(a, b, wsem.at[4 + i]) for i, (a, b) in enumerate(copies)]
    for load in small:
        load.start()
    loads = [
        pltpu.make_async_copy(wk_hbm, wkv.at[pl.ds(0, 64)], wsem.at[0]),
        pltpu.make_async_copy(wv_hbm, wkv.at[pl.ds(64, 64)], wsem.at[1]),
        pltpu.make_async_copy(wq_hbm, wq, wsem.at[2]),
        pltpu.make_async_copy(wo_hbm, wo, wsem.at[3]),
    ]
    for load in loads[:2]:
        load.start()

    sends = []

    def send(src, dst, ssem, rsem, to, group=None):
        cp = remote(src, dst, ssem, rsem, dp if group is None else group, to)
        cp.start()
        sends.append(cp)

    def arrived(dst, ssem, rsem):
        remote(dst, dst, ssem, rsem, dp, me).wait_recv()

    small[0].wait()
    own = hid[me].astype(f32)
    square = own * own
    high = square.astype(bf16)
    low = (square - high.astype(f32)).astype(bf16)
    ones = jnp.ones((8, SHARD), bf16)
    ss_send[...] = nt(ones, high) + nt(ones, low)
    ssr[me] = ss_send[...]
    for load in small[1:]:
        load.wait()
    docs[...] = jnp.transpose(jnp.broadcast_to(doc_ref[...].astype(f32), (128, TOK)))

    pl.semaphore_wait(barrier, len(PEERS) + N_DP - 1)
    for rel in FAR:
        i = ridx(rel)
        send(ss_send, ssr.at[me], sss.at[i], ssrs.at[i], peer(me, rel))

    def piece(buf, owner, rows):
        start, size = ROWS[rows]
        return buf.at[peer(me, owner + (0,)), pl.ds(start, size)]

    def move(buf, ssem, rsem, k):
        owner, rows, way = MOVES[k]
        ref = piece(buf, owner, rows)
        send(ref, ref, ssem.at[k], rsem.at[k], peer(me, way + (0,)))

    def moved(buf, ssem, rsem, k):
        owner, rows, way = MOVES[k]
        arrived(piece(buf, minus(owner, way), rows), ssem.at[k], rsem.at[k])

    def forward(buf, ssem, rsem, owner, half):
        i = (owner[0] * N_Z + owner[1]) * 2 + half
        ref = piece(buf, owner, "AB"[half])
        send(ref, ref, ssem.at[i], rsem.at[i], sibling)

    def gather(buf, ssem, rsem, fssem, frsem, use_half, use_block, before):
        ready = [((0, 0), c, h) for c in range(N_C) for h in range(2)]
        done = set()

        def run(count):
            for owner, core, half in ready[:count]:
                j = peer(me, owner + (core,))
                if core == 1:
                    i = (owner[0] * N_Z + owner[1]) * 2 + half
                    arrived(buf.at[j, pl.ds(*ROWS["AB"[half]])], fssem.at[i], frsem.at[i])
                use_half(j, half)
                done.add((owner, core, half))
                if (owner, core, 1 - half) in done:
                    use_block(j)
            del ready[:count]

        for step, (waits, starts, halves) in enumerate(EVENTS):
            for k in waits:
                moved(buf, ssem, rsem, k)
            for k in starts:
                move(buf, ssem, rsem, k)
            for owner, half in halves:
                forward(buf, fssem, frsem, owner, half)
            if before is not None and step < 2:
                ready += [(owner, core, half) for core in range(N_C) for owner, half in halves]
                continue
            if before is not None and step == 2:
                before()
            run(2 * len(halves) + (4 if 2 <= step < 8 and before is not None else 0))
            ready += [(owner, core, half) for core in range(N_C) for owner, half in halves]
        run(len(ready))

    for k in (0, 2, 3, 1, 4, 5):
        move(hid, hs, hr, k)
    for half in range(2):
        forward(hid, hfs, hfr, (0, 0), half)
    kvacc[...] = jnp.zeros_like(kvacc)
    qacc[...] = jnp.zeros_like(qacc)

    def lanes_of(j):
        return pl.ds(pl.multiple_of(j * SHARD, SHARD), SHARD)

    def clip(j, half):
        lanes = lanes_of(j)
        thresh = base_ref[:, lanes] * (1.0 + pct_ref[:, lanes].astype(f32) / 32.0)
        over = gain_ref[:, lanes] / thresh
        step = step_ref[:, lanes]

        start, size = ROWS["AB"[half]]
        rows = pl.ds(start, size)
        rest = pl.ds(TOK + start, size)
        x = hid[j, rows, :].astype(f32)
        scale = rs[rows, :]
        for l in range(SHARD // 128):
            cut = slice(l * 128, l * 128 + 128)
            ratio = x[:, cut] * scale * over[:, cut]
            bent = jnp.tanh(ratio)
            xs[j, rows, cut] = (thresh[:, cut] * bent).astype(bf16)
            slope = bent - ratio * (1.0 - bent * bent)
            slopes[j, rows, cut] = slope
            xs[j, rest, cut] = (slope * step[:, cut]).astype(bf16)

    def project(j):
        kvacc[...] += nt(xs[j], wkv[:, lanes_of(j)])


    def norms():
        for rel in PEERS:
            i = ridx(rel)
            arrived(ssr.at[source(me, rel)], sss.at[i], ssrs.at[i])
        total = jnp.sum(ssr[...], axis=0)
        scale = lax.rsqrt(total / WIDTH + EPSILON)
        rs[...] = jnp.transpose(jnp.broadcast_to(scale[0:1, :], (128, TOK)))

        for load in loads[2:]:
            load.start()
        for load in loads[:2]:
            load.wait()

    gather(hid, hs, hr, hfs, hfr, clip, project, norms)

    kvt[...] = nt(permutation(), kvacc[...].astype(bf16)).astype(bf16)

    def block(chip):
        return pl.ds(pl.multiple_of(chip * 16, 16), 16)

    kvr[me] = kvt[block(me // N_C), :]
    for rel in FAR:
        i = ridx(rel)
        to = peer(me, rel)
        send(kvt.at[block(to // N_C)], kvr.at[me], kvs.at[i], kvrs.at[i], to)

    def query_four(r, carry):
        value = qacc[...]
        for i in range(4):
            j = r * 4 + i
            value = value + jnp.dot(xs[j], wq[lanes_of(j), :], preferred_element_type=f32)
        qacc[...] = value
        return carry

    loads[2].wait()
    early = len(sends) - len(PEERS)
    lax.fori_loop(0, N_T // 4, query_four, 0)
    for cp in sends[:early]:
        cp.wait_send()
    del sends[:early]
    for h in range(HEADS):
        cut = slice(h * 128, h * 128 + 128)
        for out, top in ((qp, 0), (qt, TOK)):
            z = qacc[pl.ds(top, TOK), cut]
            out[:, cut] = (z * cos_ref[...] + pltpu.roll(z, 64, 1) * sin_ref[...]).astype(bf16)

    for rel in PEERS:
        i = ridx(rel)
        arrived(kvr.at[source(me, rel)], kvs.at[i], kvrs.at[i])
    both = kvr[...].astype(f32)
    keys = both[:, 0:8, :].reshape(HEAD_DIM, 2 * TOK)
    vals = both[:, 8:16, :].reshape(HEAD_DIM, 2 * TOK).astype(bf16)
    vp[...] = vals[:, :TOK]
    vt[...] = vals[:, TOK:]
    cost, sint = cost_ref[...], sint_ref[...]
    for out, left in ((kp, 0), (kt, TOK)):
        z = keys[:, left : left + TOK]
        front, back = z[:64], z[64:]
        out[0:64, :] = (front * cost - back * sint).astype(bf16)
        out[64:128, :] = (back * cost + front * sint).astype(bf16)

    same = jnp.concatenate([docs[...], docs[...]], axis=1) == doc_ref[...].astype(f32)
    place = lax.broadcasted_iota(jnp.int32, (TOK, TOK), 0) >= lax.broadcasted_iota(jnp.int32, (TOK, TOK), 1)
    allowed = same & place
    score_scale = HEAD_DIM ** (-0.5)

    def dot(a, b):
        return jnp.dot(a, b, preferred_element_type=f32)

    for h in range(HEADS):
        cut = slice(h * 128, h * 128 + 128)
        q0, q1 = qp[:, cut], qt[:, cut]
        scores = jnp.where(allowed, dot(q0, kp[...]) * score_scale, MASKED)
        grown = jnp.exp(scores - jnp.max(scores, axis=1, keepdims=True))
        prob = grown / jnp.sum(grown, axis=1, keepdims=True)
        probs[h] = prob
        t = (dot(q1, kp[...]) + dot(q0, kt[...])) * score_scale
        tan = (prob * (t - jnp.sum(prob * t, axis=1, keepdims=True))).astype(bf16)
        ctx[:, cut] = (nt(tan, vp[...]) + nt(prob.astype(bf16), vt[...])).astype(bf16)

    loads[3].wait()

    def slot(chip):
        return chip[0] * N_Z + chip[1]

    def pair_part(s):
        i = slot(PARTS[s])
        pair_out[i] = dot(ctx[...], wo[:, lanes_of(peer(me, PARTS[s] + (1,)))]).astype(bf16)
        send(pair_out.at[i], pair_in.at[i], ps.at[i], pr.at[i], sibling)

    def give(k):
        chip, rows, way = SUMS[k]
        start, size = ROWS[rows]
        send(part.at[slot(chip), pl.ds(start, size)], sums.at[k, pl.ds(0, size)], qs.at[k], qr.at[k], peer(me, way + (0,)))

    def own_part(s):
        i = slot(PARTS[s])
        mine = dot(ctx[...], wo[:, lanes_of(peer(me, PARTS[s] + (0,)))]).astype(bf16).astype(f32)
        arrived(pair_in.at[i], ps.at[i], pr.at[i])
        part[i] = (mine + pair_in[i].astype(f32)).astype(bf16)
        for k in FIRST.get(PARTS[s], ()):
            give(k)

    def add(rows, into, *parts):
        chip, out = into
        start, size = ROWS[rows]
        for k in parts:
            arrived(sums.at[k, pl.ds(0, ROWS[SUMS[k][1]][1])], qs.at[k], qr.at[k])
        value = part[slot(chip), pl.ds(start, size), :].astype(f32)
        for k in parts:
            low = start - ROWS[SUMS[k][1]][0]
            value = value + sums[k, pl.ds(low, size), :].astype(f32)
        if out is None:
            part[slot(chip), pl.ds(start, size), :] = value.astype(bf16)
        else:
            out[me, pl.ds(start, size), :] = value.astype(bf16)

    def take(rows, chip, *parts):
        add(rows, (chip, None), *parts)

    pair_part(0)
    pair_part(1)
    for s in range(8):
        if s + 2 < 8:
            pair_part(s + 2)
        own_part(s)
        if s == 5:
            take("2", (1, 3), 3)
            give(10)
            take("3", (1, 1), 4)
            give(9)
    take("A", (0, 2), 0)
    give(5)
    give(6)
    take("2", (0, 3), 7)
    give(16)
    take("3", (0, 1), 8)
    give(15)
    take("B", (1, 0), 9, 10)
    give(12)
    take("1", (0, 1), 6)
    take("A", (0, 1), 1)
    give(13)
    take("0", (0, 3), 5)
    take("A", (0, 3), 2)
    give(14)
    add("B", ((0, 0), tg), 12, 15, 16)
    move(tg, gs, gr, 0)
    add("A", ((0, 0), tg), 11, 13, 14)
    for k in (2, 3, 1, 4, 5):
        move(tg, gs, gr, k)
    for half in range(2):
        forward(tg, gfs, gfr, (0, 0), half)
    result = pltpu.make_async_copy(tg.at[me], out_hbm, wsem.at[0])
    result.start()
    bacc[...] = jnp.zeros_like(bacc)

    def back(j):
        bacc[...] += nt(tg[j], wo[:, lanes_of(j)])

    gather(tg, gs, gr, gfs, gfr, lambda j, half: None, back, None)

    gk = jnp.zeros((HEAD_DIM, TOK), f32)
    gv = jnp.zeros((HEAD_DIM, TOK), f32)
    marks = []
    for h in range(HEADS):
        cut = slice(h * 128, h * 128 + 128)
        bc = bacc[:, cut].astype(bf16)
        prob = probs[h]
        g = dot(bc, vp[...])
        score = (prob * (g - jnp.sum(prob * g, axis=1, keepdims=True)) * score_scale).astype(bf16)
        marks.append(score)
        gk = gk + tn(qp[:, cut], score)
        gv = gv + tn(bc, prob.astype(bf16))
    front, back_half = gk[:64], gk[64:]
    gk = jnp.concatenate([front * cost + back_half * sint, back_half * cost - front * sint], axis=0)
    gkv_out[...] = jnp.concatenate([gk.reshape(N_T, 8, TOK), gv.reshape(N_T, 8, TOK)], axis=1).astype(bf16)
    for rel in FAR:
        i = ridx(rel)
        to = peer(me, rel)
        send(gkv_out.at[to], gkv_in.at[me], ks.at[i], kr.at[i], to)
    gkv_in[me] = gkv_out[me]
    early = len(sends) - len(PEERS)
    for h in range(HEADS):
        cut = slice(h * 128, h * 128 + 128)
        z = nt(marks[h], kp[...])
        gq[:, cut] = (z * cos_ref[...] - pltpu.roll(z, 64, 1) * sin_ref[...]).astype(bf16)

    def column_sums(product):
        line = jnp.sum(product, axis=0, keepdims=True)
        return jnp.concatenate([line[:, l * 128 : l * 128 + 128] for l in range(4)] * 2, axis=0)

    def query_step(j, carry):
        gnv[j] = column_sums(nt(gq[...], wq[lanes_of(j), :]) * slopes[j])
        return carry

    lax.fori_loop(0, N_T, query_step, 0, unroll=4)
    for cp in sends[:early]:
        cp.wait_send()
    del sends[:early]
    for rel in PEERS:
        i = ridx(rel)
        arrived(gkv_in.at[source(me, rel)], ks.at[i], kr.at[i])
    pairs = gkv_in[...].astype(f32).reshape(N_T // 2, 2, 16, TOK)
    summed = (pairs[:, 0] + pairs[:, 1]).reshape(HEAD_DIM, TOK).astype(bf16)
    gkv[...] = tn(summed, permutation()).astype(bf16)

    def key_step(j, carry):
        gnv[j] += column_sums(dot(gkv[...], wkv[:, lanes_of(j)]) * slopes[j])
        return carry

    for group in (FAR[:8], FAR[8:]):
        for rel in group:
            key_step(peer(me, rel), 0)
        for rel in group:
            i = ridx(rel)
            to = peer(me, rel)
            send(gnv.at[to], gnv_in.at[me], ns.at[i], nr.at[i], to)
    key_step(me, 0)
    gnv_in[me] = gnv[me]
    early = len(sends) - len(PEERS)
    for cp in sends[:early]:
        cp.wait_send()
    del sends[:early]
    for rel in PEERS:
        i = ridx(rel)
        arrived(gnv_in.at[source(me, rel)], ns.at[i], nr.at[i])
    dpv[...] = jnp.sum(gnv_in[...], axis=0)
    dpv_in[dp] = dpv[...]
    for d in (5, 3, 4, 2, 6, 7, 1):
        send(dpv, dpv_in.at[dp], ds.at[d], dr.at[d], me, (dp + d) % N_DP)
    early = len(sends) - N_DP + 1
    for cp in sends[:early]:
        cp.wait_send()
    del sends[:early]
    result.wait()
    for d in range(1, N_DP):
        arrived(dpv_in.at[(dp + N_DP - d) % N_DP], ds.at[d], dr.at[d])
    gn_ref[...] = jnp.sum(dpv_in[...], axis=0)[0:4, :]
    for cp in sends:
        cp.wait_send()


VM = pl.BlockSpec(memory_space=pltpu.VMEM)
ANY = pl.BlockSpec(memory_space=pl.ANY)


def whole(*operands):
    sds = jax.ShapeDtypeStruct
    sem = pltpu.SemaphoreType.DMA((18,))
    vm = pltpu.VMEM
    return pl.pallas_call(
        body,
        name="block",
        out_shape=[sds((TOK, SHARD), bf16), sds((4, 128), f32)],
        in_specs=[ANY] * 14,
        out_specs=[ANY, VM],
        scratch_shapes=[
            vm((1, WIDTH), f32),
            vm((1, WIDTH), f32),
            vm((1, WIDTH), jnp.int32),
            vm((1, WIDTH), f32),
            vm((1, TOK), jnp.int32),
            vm((TOK, 128), f32),
            vm((TOK, 128), f32),
            vm((64, TOK), f32),
            vm((64, TOK), f32),
            vm((N_T, TOK, SHARD), bf16),
            vm((N_T, 2 * TOK, SHARD), bf16),
            vm((N_T, TOK, SHARD), f32),
            vm((WIDTH, SHARD), bf16),
            vm((128, WIDTH), bf16),
            vm((SHARD, WIDTH), bf16),
            vm((8, TOK), f32),
            vm((N_T, 8, TOK), f32),
            vm((TOK, 128), f32),
            vm((2 * TOK, 128), f32),
            vm((2 * TOK, SHARD), f32),
            vm((128, 2 * TOK), bf16),
            vm((N_T, 16, 2 * TOK), bf16),
            vm((TOK, SHARD), bf16),
            vm((TOK, SHARD), bf16),
            vm((HEAD_DIM, TOK), bf16),
            vm((HEAD_DIM, TOK), bf16),
            vm((HEAD_DIM, TOK), bf16),
            vm((HEAD_DIM, TOK), bf16),
            vm((TOK, 128), f32),
            vm((HEADS, TOK, TOK), f32),
            vm((TOK, SHARD), bf16),
            vm((8, TOK, SHARD), bf16),
            vm((8, TOK, SHARD), bf16),
            vm((8, TOK, SHARD), bf16),
            vm((len(SUMS), 144, SHARD), bf16),
            vm((N_T, TOK, SHARD), bf16),
            vm((TOK, SHARD), f32),
            vm((TOK, SHARD), bf16),
            vm((N_T, 16, TOK), bf16),
            vm((N_T, 16, TOK), bf16),
            vm((TOK, 128), bf16),
            vm((N_T, 8, 128), f32),
            vm((N_T, 8, 128), f32),
            vm((8, 128), f32),
            vm((N_DP, 8, 128), f32),
            pltpu.SemaphoreType.DMA((14,)),
        ]
        + [sem] * 22,
        compiler_params=pltpu.CompilerParams(collective_id=1, has_side_effects=True, vmem_limit_bytes=VMEM_BYTES),
    )(*operands)


def finish_body(shard_ref, gn_ref, out_ref, mean_ref):
    out_ref[...] = shard_ref[...]
    mean_ref[...] = gn_ref[...] / (TOK * N_DP)


def finish(shard, gn):
    sds = jax.ShapeDtypeStruct
    return pl.pallas_call(
        finish_body,
        name="finish",
        out_shape=[sds((TOK, SHARD), bf16), sds((4, 128), f32)],
        in_specs=[VM] * 2,
        out_specs=[VM] * 2,
    )(shard, gn)


def tables():
    positions = np.arange(TOK, dtype=np.float32)
    frequency = np.exp(np.float32(-math.log(ROPE_BASE) * 2.0) * np.arange(64, dtype=np.float32) / np.float32(HEAD_DIM))
    angles = positions[:, None] * frequency[None, :].astype(np.float32)
    cosine, sine = np.cos(angles), np.sin(angles)
    return (
        np.concatenate([cosine, cosine], axis=1),
        np.concatenate([-sine, sine], axis=1),
        np.ascontiguousarray(cosine.T),
        np.ascontiguousarray(sine.T),
    )


def on_device(
    hidden_in, norm_gain, clip_base, pct_index, clip_step, w_query, w_key, w_value, w_out, doc_ids
):
    row = lambda v: v.reshape(1, WIDTH)
    tangent_shard, gn = whole(
        hidden_in, row(norm_gain), row(clip_base), row(pct_index), row(clip_step), doc_ids,
        *(jnp.asarray(t) for t in tables()),
        w_query, w_key.T, w_value.T, w_out,
    )
    tangent_shard, gn = finish(tangent_shard, gn)
    return (tangent_shard, gn.reshape(SHARD))


def solution(mesh):
    in_specs = (
        P("dp", "tensor"),
        P(),
        P(),
        P(),
        P(),
        P(None, "tensor"),
        P(None, "tensor"),
        P(None, "tensor"),
        P("tensor", None),
        P("dp", None),
    )
    out_specs = (P("dp", "tensor"), P("tensor"))
    return jax.shard_map(
        on_device, mesh=mesh, in_specs=in_specs, out_specs=out_specs, check_vma=False
    )
```

```python
import functools
import math

import jax
import jax.numpy as jnp
import numpy as np
from jax import lax
from jax.experimental import pallas as pl
from jax.experimental.pallas import tpu as pltpu
from jax.sharding import PartitionSpec as P

HEAD_DIM = 128
EPSILON = 1e-05
ROPE_BASE = 500000.0
MASKED = -1e30
MESH = pl.DeviceIdType.MESH
f32 = jnp.float32
bf16 = jnp.bfloat16

N_Y, N_Z, N_C = 2, 4, 2
N_T = N_Y * N_Z * N_C
TOK = 256
SHARD = 512
WIDTH = N_T * SHARD
HEADS = 4
N_DP = 8
VMEM_BYTES = 60 << 20
HALF = TOK // 2

RELS = [(dy, dz, dc) for dy in range(N_Y) for dz in range(N_Z) for dc in range(N_C)]
PEERS = [r for r in RELS if r != (0, 0, 0)]
ROWS = {"A": (0, 112), "B": (112, 144), "0": (0, 48), "1": (48, 64), "2": (112, 80), "3": (192, 64)}
Y, ZP, ZM = (1, 0), (0, 1), (0, 3)

MOVES = [
    ((0, 0), "B", Y), ((0, 0), "A", Y), ((0, 0), "A", ZP), ((0, 0), "A", ZM), ((0, 0), "B", ZP), ((0, 0), "B", ZM),
    ((0, 3), "0", ZP), ((0, 1), "1", ZM), ((0, 3), "2", ZP), ((0, 1), "3", ZM), ((0, 3), "A", Y), ((0, 1), "A", Y),
    ((1, 0), "B", ZP), ((1, 0), "B", ZM), ((1, 3), "2", ZP), ((1, 1), "3", ZM), ((0, 2), "0", Y), ((0, 2), "1", Y),
]
EVENTS = [
    ([0], [12, 13], [((1, 0), 1)]),
    ([2], [10, 6], [((0, 3), 0)]),
    ([3], [11, 7], [((0, 1), 0)]),
    ([1], [], [((1, 0), 0)]),
    ([4], [8], [((0, 3), 1)]),
    ([5], [9], [((0, 1), 1)]),
    ([6], [16], []),
    ([7], [17], [((0, 2), 0)]),
    ([12], [14], [((1, 3), 1)]),
    ([13], [15], [((1, 1), 1)]),
    ([8, 9], [], [((0, 2), 1)]),
    ([10, 11], [], [((1, 3), 0), ((1, 1), 0)]),
    ([14, 15], [], [((1, 2), 1)]),
    ([16, 17], [], [((1, 2), 0)]),
]
SUMS = [
    ((1, 2), "A", Y), ((1, 1), "A", Y), ((1, 3), "A", Y), ((1, 2), "2", ZM), ((1, 2), "3", ZP),
    ((0, 2), "0", ZM), ((0, 2), "1", ZP), ((0, 2), "2", ZM), ((0, 2), "3", ZP), ((1, 1), "B", ZP), ((1, 3), "B", ZM),
    ((1, 0), "A", Y), ((1, 0), "B", Y), ((0, 1), "A", ZP), ((0, 3), "A", ZM), ((0, 1), "B", ZP), ((0, 3), "B", ZM),
]
PARTS = [(1, 2), (1, 1), (1, 3), (0, 2), (1, 0), (0, 1), (0, 3), (0, 0)]
FIRST = {(1, 2): [0, 3, 4], (1, 1): [1], (1, 3): [2], (0, 2): [7, 8], (1, 0): [11]}

FAR = [chip + (core,) for chip in PARTS for core in (1, 0)][:-1]


def minus(a, b):
    return ((a[0] - b[0]) % N_Y, (a[1] - b[1]) % N_Z)


def ridx(rel):
    return (rel[0] * N_Z + rel[1]) * N_C + rel[2]


def peer(me, rel):
    y, z, c = me // (N_Z * N_C), (me // N_C) % N_Z, me % N_C
    y = (y + rel[0]) % N_Y
    z = (z + rel[1]) % N_Z
    c = (c + rel[2]) % N_C
    return (y * N_Z + z) * N_C + c


def source(me, rel):
    return peer(me, (-rel[0], -rel[1], -rel[2]))


def remote(src, dst, ssem, rsem, dp, target):
    return pltpu.make_async_remote_copy(
        src_ref=src, dst_ref=dst, send_sem=ssem, recv_sem=rsem, device_id=(dp, target), device_id_type=MESH
    )


def nt(a, b):
    return lax.dot_general(a, b, (((1,), (1,)), ((), ())), preferred_element_type=f32)


def tn(a, b):
    return lax.dot_general(a, b, (((0,), (0,)), ((), ())), preferred_element_type=f32)


def permutation():
    row = lax.broadcasted_iota(jnp.int32, (128, 128), 0)
    col = lax.broadcasted_iota(jnp.int32, (128, 128), 1)
    head, low = row // 16, row % 16
    want = jnp.where(low < 8, low * 8 + head, 64 + (low - 8) * 8 + head)
    return (col == want).astype(f32).astype(bf16)


def body(
    x_hbm, gain_hbm, base_hbm, pct_hbm, step_hbm, doc_hbm, cos_hbm, sin_hbm, cost_hbm, sint_hbm,
    wq_hbm, wk_hbm, wv_hbm, wo_hbm,
    out_hbm, gn_ref,
    gain_ref, base_ref, pct_ref, step_ref, doc_ref, cos_ref, sin_ref, cost_ref, sint_ref,
    hid, xs, slopes, wq, wkv, wo, ss_send, ssr, rs, kvacc, qacc, kvt, kvr, qp, qt, kp, kt, vp, vt, docs, probs, ctx,
    pair_out, pair_in, part, sums, tg, bacc, gq, gkv_out, gkv_in, gkv, gnv, gnv_in, dpv, dpv_in,
    wsem, hs, hr, hfs, hfr, sss, ssrs, kvs, kvrs, ps, pr, qs, qr, gs, gr, gfs, gfr, ks, kr, ns, nr, ds, dr,
):
    me = lax.axis_index("tensor")
    dp = lax.axis_index("dp")
    sibling = peer(me, (0, 0, 1))
    barrier = pltpu.get_barrier_semaphore()
    for rel in PEERS:
        pl.semaphore_signal(barrier, inc=1, device_id=(dp, peer(me, rel)), device_id_type=MESH)
    for d in range(1, N_DP):
        pl.semaphore_signal(barrier, inc=1, device_id=((dp + d) % N_DP, me), device_id_type=MESH)
    copies = [
        (x_hbm, hid.at[me]), (doc_hbm, doc_ref), (gain_hbm, gain_ref), (base_hbm, base_ref), (pct_hbm, pct_ref),
        (step_hbm, step_ref), (cos_hbm, cos_ref), (sin_hbm, sin_ref), (cost_hbm, cost_ref), (sint_hbm, sint_ref),
    ]
    small = [pltpu.make_async_copy(a, b, wsem.at[4 + i]) for i, (a, b) in enumerate(copies)]
    for load in small:
        load.start()
    loads = [
        pltpu.make_async_copy(wk_hbm, wkv.at[pl.ds(0, 64)], wsem.at[0]),
        pltpu.make_async_copy(wv_hbm, wkv.at[pl.ds(64, 64)], wsem.at[1]),
        pltpu.make_async_copy(wq_hbm, wq, wsem.at[2]),
        pltpu.make_async_copy(wo_hbm, wo, wsem.at[3]),
    ]
    for load in loads[:2]:
        load.start()

    sends = []

    def send(src, dst, ssem, rsem, to, group=None):
        cp = remote(src, dst, ssem, rsem, dp if group is None else group, to)
        cp.start()
        sends.append(cp)

    def arrived(dst, ssem, rsem):
        remote(dst, dst, ssem, rsem, dp, me).wait_recv()

    small[0].wait()
    own = hid[me].astype(f32)
    square = own * own
    high = square.astype(bf16)
    low = (square - high.astype(f32)).astype(bf16)
    ones = jnp.ones((8, SHARD), bf16)
    ss_send[...] = nt(ones, high) + nt(ones, low)
    ssr[me] = ss_send[...]
    for load in small[1:]:
        load.wait()
    docs[...] = jnp.transpose(jnp.broadcast_to(doc_ref[...].astype(f32), (128, TOK)))

    pl.semaphore_wait(barrier, len(PEERS) + N_DP - 1)
    for rel in FAR:
        i = ridx(rel)
        send(ss_send, ssr.at[me], sss.at[i], ssrs.at[i], peer(me, rel))

    def piece(buf, owner, rows):
        start, size = ROWS[rows]
        return buf.at[peer(me, owner + (0,)), pl.ds(start, size)]

    def move(buf, ssem, rsem, k):
        owner, rows, way = MOVES[k]
        ref = piece(buf, owner, rows)
        send(ref, ref, ssem.at[k], rsem.at[k], peer(me, way + (0,)))

    def moved(buf, ssem, rsem, k):
        owner, rows, way = MOVES[k]
        arrived(piece(buf, minus(owner, way), rows), ssem.at[k], rsem.at[k])

    def forward(buf, ssem, rsem, owner, half):
        i = (owner[0] * N_Z + owner[1]) * 2 + half
        ref = piece(buf, owner, "AB"[half])
        send(ref, ref, ssem.at[i], rsem.at[i], sibling)

    def gather(buf, ssem, rsem, fssem, frsem, use_half, use_block, before):
        ready = [((0, 0), c, h) for c in range(N_C) for h in range(2)]
        done = set()

        def run(count):
            for owner, core, half in ready[:count]:
                j = peer(me, owner + (core,))
                if core == 1:
                    i = (owner[0] * N_Z + owner[1]) * 2 + half
                    arrived(buf.at[j, pl.ds(*ROWS["AB"[half]])], fssem.at[i], frsem.at[i])
                use_half(j, half)
                done.add((owner, core, half))
                if (owner, core, 1 - half) in done:
                    use_block(j)
            del ready[:count]

        for step, (waits, starts, halves) in enumerate(EVENTS):
            for k in waits:
                moved(buf, ssem, rsem, k)
            for k in starts:
                move(buf, ssem, rsem, k)
            for owner, half in halves:
                forward(buf, fssem, frsem, owner, half)
            if before is not None and step < 2:
                ready += [(owner, core, half) for core in range(N_C) for owner, half in halves]
                continue
            if before is not None and step == 2:
                before()
            run(2 * len(halves) + (4 if 2 <= step < 8 and before is not None else 0))
            ready += [(owner, core, half) for core in range(N_C) for owner, half in halves]
        run(len(ready))

    for k in (0, 2, 3, 1, 4, 5):
        move(hid, hs, hr, k)
    for half in range(2):
        forward(hid, hfs, hfr, (0, 0), half)
    kvacc[...] = jnp.zeros_like(kvacc)
    qacc[...] = jnp.zeros_like(qacc)

    def lanes_of(j):
        return pl.ds(pl.multiple_of(j * SHARD, SHARD), SHARD)

    def clip(j, half):
        lanes = lanes_of(j)
        thresh = base_ref[:, lanes] * (1.0 + pct_ref[:, lanes].astype(f32) / 32.0)
        over = gain_ref[:, lanes] / thresh
        step = step_ref[:, lanes]

        start, size = ROWS["AB"[half]]
        rows = pl.ds(start, size)
        rest = pl.ds(TOK + start, size)
        x = hid[j, rows, :].astype(f32)
        scale = rs[rows, :]
        for l in range(SHARD // 128):
            cut = slice(l * 128, l * 128 + 128)
            ratio = x[:, cut] * scale * over[:, cut]
            bent = jnp.tanh(ratio)
            xs[j, rows, cut] = (thresh[:, cut] * bent).astype(bf16)
            slope = bent - ratio * (1.0 - bent * bent)
            slopes[j, rows, cut] = slope
            xs[j, rest, cut] = (slope * step[:, cut]).astype(bf16)

    def project(j):
        kvacc[...] += nt(xs[j], wkv[:, lanes_of(j)])


    def norms():
        for rel in PEERS:
            i = ridx(rel)
            arrived(ssr.at[source(me, rel)], sss.at[i], ssrs.at[i])
        total = jnp.sum(ssr[...], axis=0)
        scale = lax.rsqrt(total / WIDTH + EPSILON)
        rs[...] = jnp.transpose(jnp.broadcast_to(scale[0:1, :], (128, TOK)))

        for load in loads[2:]:
            load.start()
        for load in loads[:2]:
            load.wait()

    gather(hid, hs, hr, hfs, hfr, clip, project, norms)

    kvt[...] = nt(permutation(), kvacc[...].astype(bf16)).astype(bf16)

    def block(chip):
        return pl.ds(pl.multiple_of(chip * 16, 16), 16)

    kvr[me] = kvt[block(me // N_C), :]
    for rel in FAR:
        i = ridx(rel)
        to = peer(me, rel)
        send(kvt.at[block(to // N_C)], kvr.at[me], kvs.at[i], kvrs.at[i], to)

    def query_four(r, carry):
        value = qacc[...]
        for i in range(4):
            j = r * 4 + i
            value = value + jnp.dot(xs[j], wq[lanes_of(j), :], preferred_element_type=f32)
        qacc[...] = value
        return carry

    loads[2].wait()
    early = len(sends) - len(PEERS)
    lax.fori_loop(0, N_T // 4, query_four, 0)
    for cp in sends[:early]:
        cp.wait_send()
    del sends[:early]
    for h in range(HEADS):
        cut = slice(h * 128, h * 128 + 128)
        for out, top in ((qp, 0), (qt, TOK)):
            z = qacc[pl.ds(top, TOK), cut]
            out[:, cut] = (z * cos_ref[...] + pltpu.roll(z, 64, 1) * sin_ref[...]).astype(bf16)

    for rel in PEERS:
        i = ridx(rel)
        arrived(kvr.at[source(me, rel)], kvs.at[i], kvrs.at[i])
    both = kvr[...].astype(f32)
    keys = both[:, 0:8, :].reshape(HEAD_DIM, 2 * TOK)
    vals = both[:, 8:16, :].reshape(HEAD_DIM, 2 * TOK).astype(bf16)
    vp[...] = vals[:, :TOK]
    vt[...] = vals[:, TOK:]
    cost, sint = cost_ref[...], sint_ref[...]
    for out, left in ((kp, 0), (kt, TOK)):
        z = keys[:, left : left + TOK]
        front, back = z[:64], z[64:]
        out[0:64, :] = (front * cost - back * sint).astype(bf16)
        out[64:128, :] = (back * cost + front * sint).astype(bf16)

    def allowed(t):
        n = HALF * (t + 1)
        same = jnp.concatenate([docs[pl.ds(t * HALF, HALF), :]] * (t + 1), axis=1) == doc_ref[:, 0:n].astype(f32)
        row = lax.broadcasted_iota(jnp.int32, (HALF, n), 0) + t * HALF
        return same & (row >= lax.broadcasted_iota(jnp.int32, (HALF, n), 1))

    masks = [allowed(0), allowed(1)]
    score_scale = HEAD_DIM ** (-0.5)

    def dot(a, b):
        return jnp.dot(a, b, preferred_element_type=f32)

    for h in range(HEADS):
        cut = slice(h * 128, h * 128 + 128)
        for t in range(2):
            rows, n = pl.ds(t * HALF, HALF), HALF * (t + 1)
            q0, q1 = qp[rows, cut], qt[rows, cut]
            k0 = kp[:, 0:n]
            scores = jnp.where(masks[t], dot(q0, k0) * score_scale, MASKED)
            grown = jnp.exp(scores - jnp.max(scores, axis=1, keepdims=True))
            prob = grown / jnp.sum(grown, axis=1, keepdims=True)
            probs[h, rows, 0:n] = prob
            tan = (dot(q1, k0) + dot(q0, kt[:, 0:n])) * score_scale
            tan = (prob * (tan - jnp.sum(prob * tan, axis=1, keepdims=True))).astype(bf16)
            ctx[rows, cut] = (nt(tan, vp[:, 0:n]) + nt(prob.astype(bf16), vt[:, 0:n])).astype(bf16)

    loads[3].wait()

    def slot(chip):
        return chip[0] * N_Z + chip[1]

    def pair_part(s):
        i = slot(PARTS[s])
        pair_out[i] = dot(ctx[...], wo[:, lanes_of(peer(me, PARTS[s] + (1,)))]).astype(bf16)
        send(pair_out.at[i], pair_in.at[i], ps.at[i], pr.at[i], sibling)

    def give(k):
        chip, rows, way = SUMS[k]
        start, size = ROWS[rows]
        send(part.at[slot(chip), pl.ds(start, size)], sums.at[k, pl.ds(0, size)], qs.at[k], qr.at[k], peer(me, way + (0,)))

    def own_part(s):
        i = slot(PARTS[s])
        mine = dot(ctx[...], wo[:, lanes_of(peer(me, PARTS[s] + (0,)))]).astype(bf16).astype(f32)
        arrived(pair_in.at[i], ps.at[i], pr.at[i])
        part[i] = (mine + pair_in[i].astype(f32)).astype(bf16)
        for k in FIRST.get(PARTS[s], ()):
            give(k)

    def add(rows, into, *parts):
        chip, out = into
        start, size = ROWS[rows]
        for k in parts:
            arrived(sums.at[k, pl.ds(0, ROWS[SUMS[k][1]][1])], qs.at[k], qr.at[k])
        value = part[slot(chip), pl.ds(start, size), :].astype(f32)
        for k in parts:
            low = start - ROWS[SUMS[k][1]][0]
            value = value + sums[k, pl.ds(low, size), :].astype(f32)
        if out is None:
            part[slot(chip), pl.ds(start, size), :] = value.astype(bf16)
        else:
            out[me, pl.ds(start, size), :] = value.astype(bf16)

    def take(rows, chip, *parts):
        add(rows, (chip, None), *parts)

    pair_part(0)
    pair_part(1)
    for s in range(8):
        if s + 2 < 8:
            pair_part(s + 2)
        own_part(s)
        if s == 5:
            take("2", (1, 3), 3)
            give(10)
            take("3", (1, 1), 4)
            give(9)
    take("A", (0, 2), 0)
    give(5)
    give(6)
    take("2", (0, 3), 7)
    give(16)
    take("3", (0, 1), 8)
    give(15)
    take("B", (1, 0), 9, 10)
    give(12)
    take("1", (0, 1), 6)
    take("A", (0, 1), 1)
    give(13)
    take("0", (0, 3), 5)
    take("A", (0, 3), 2)
    give(14)
    add("B", ((0, 0), tg), 12, 15, 16)
    move(tg, gs, gr, 0)
    add("A", ((0, 0), tg), 11, 13, 14)
    for k in (2, 3, 1, 4, 5):
        move(tg, gs, gr, k)
    for half in range(2):
        forward(tg, gfs, gfr, (0, 0), half)
    result = pltpu.make_async_copy(tg.at[me], out_hbm, wsem.at[0])
    result.start()
    bacc[...] = jnp.zeros_like(bacc)

    def back(j):
        bacc[...] += nt(tg[j], wo[:, lanes_of(j)])

    gather(tg, gs, gr, gfs, gfr, lambda j, half: None, back, None)

    gk = [jnp.zeros((HEAD_DIM, HALF * (t + 1)), f32) for t in range(2)]
    gv = [jnp.zeros((HEAD_DIM, HALF * (t + 1)), f32) for t in range(2)]
    marks = {}
    for h in range(HEADS):
        cut = slice(h * 128, h * 128 + 128)
        for t in range(2):
            rows, n = pl.ds(t * HALF, HALF), HALF * (t + 1)
            bc = bacc[rows, cut].astype(bf16)
            prob = probs[h, rows, 0:n]
            g = dot(bc, vp[:, 0:n])
            score = (prob * (g - jnp.sum(prob * g, axis=1, keepdims=True)) * score_scale).astype(bf16)
            marks[h, t] = score
            gk[t] = gk[t] + tn(qp[rows, cut], score)
            gv[t] = gv[t] + tn(bc, prob.astype(bf16))
    gk, gv = (jnp.concatenate([v[0] + v[1][:, :HALF], v[1][:, HALF:]], axis=1) for v in (gk, gv))
    front, back_half = gk[:64], gk[64:]
    gk = jnp.concatenate([front * cost + back_half * sint, back_half * cost - front * sint], axis=0)
    gkv_out[...] = jnp.concatenate([gk.reshape(N_T, 8, TOK), gv.reshape(N_T, 8, TOK)], axis=1).astype(bf16)
    for rel in FAR:
        i = ridx(rel)
        to = peer(me, rel)
        send(gkv_out.at[to], gkv_in.at[me], ks.at[i], kr.at[i], to)
    gkv_in[me] = gkv_out[me]
    early = len(sends) - len(PEERS)
    for h in range(HEADS):
        cut = slice(h * 128, h * 128 + 128)
        for t in range(2):
            rows = pl.ds(t * HALF, HALF)
            z = nt(marks[h, t], kp[:, 0 : HALF * (t + 1)])
            gq[rows, cut] = (z * cos_ref[rows, :] - pltpu.roll(z, 64, 1) * sin_ref[rows, :]).astype(bf16)

    def column_sums(product):
        line = jnp.sum(product, axis=0, keepdims=True)
        return jnp.concatenate([line[:, l * 128 : l * 128 + 128] for l in range(4)] * 2, axis=0)

    def query_step(j, carry):
        gnv[j] = column_sums(nt(gq[...], wq[lanes_of(j), :]) * slopes[j])
        return carry

    lax.fori_loop(0, N_T, query_step, 0, unroll=4)
    for cp in sends[:early]:
        cp.wait_send()
    del sends[:early]
    for rel in PEERS:
        i = ridx(rel)
        arrived(gkv_in.at[source(me, rel)], ks.at[i], kr.at[i])
    pairs = gkv_in[...].astype(f32).reshape(N_T // 2, 2, 16, TOK)
    summed = (pairs[:, 0] + pairs[:, 1]).reshape(HEAD_DIM, TOK).astype(bf16)
    gkv[...] = tn(summed, permutation()).astype(bf16)

    def key_step(j, carry):
        gnv[j] += column_sums(dot(gkv[...], wkv[:, lanes_of(j)]) * slopes[j])
        return carry

    for group in (FAR[:8], FAR[8:]):
        for rel in group:
            key_step(peer(me, rel), 0)
        for rel in group:
            i = ridx(rel)
            to = peer(me, rel)
            send(gnv.at[to], gnv_in.at[me], ns.at[i], nr.at[i], to)
    key_step(me, 0)
    gnv_in[me] = gnv[me]
    early = len(sends) - len(PEERS)
    for cp in sends[:early]:
        cp.wait_send()
    del sends[:early]
    for rel in PEERS:
        i = ridx(rel)
        arrived(gnv_in.at[source(me, rel)], ns.at[i], nr.at[i])
    dpv[...] = jnp.sum(gnv_in[...], axis=0)
    dpv_in[dp] = dpv[...]
    for d in (5, 3, 4, 2, 6, 7, 1):
        send(dpv, dpv_in.at[dp], ds.at[d], dr.at[d], me, (dp + d) % N_DP)
    early = len(sends) - N_DP + 1
    for cp in sends[:early]:
        cp.wait_send()
    del sends[:early]
    result.wait()
    for d in range(1, N_DP):
        arrived(dpv_in.at[(dp + N_DP - d) % N_DP], ds.at[d], dr.at[d])
    gn_ref[...] = jnp.sum(dpv_in[...], axis=0)[0:4, :]
    for cp in sends:
        cp.wait_send()


VM = pl.BlockSpec(memory_space=pltpu.VMEM)
ANY = pl.BlockSpec(memory_space=pl.ANY)


def whole(*operands):
    sds = jax.ShapeDtypeStruct
    sem = pltpu.SemaphoreType.DMA((18,))
    vm = pltpu.VMEM
    return pl.pallas_call(
        body,
        name="block",
        out_shape=[sds((TOK, SHARD), bf16), sds((4, 128), f32)],
        in_specs=[ANY] * 14,
        out_specs=[ANY, VM],
        scratch_shapes=[
            vm((1, WIDTH), f32),
            vm((1, WIDTH), f32),
            vm((1, WIDTH), jnp.int32),
            vm((1, WIDTH), f32),
            vm((1, TOK), jnp.int32),
            vm((TOK, 128), f32),
            vm((TOK, 128), f32),
            vm((64, TOK), f32),
            vm((64, TOK), f32),
            vm((N_T, TOK, SHARD), bf16),
            vm((N_T, 2 * TOK, SHARD), bf16),
            vm((N_T, TOK, SHARD), f32),
            vm((WIDTH, SHARD), bf16),
            vm((128, WIDTH), bf16),
            vm((SHARD, WIDTH), bf16),
            vm((8, TOK), f32),
            vm((N_T, 8, TOK), f32),
            vm((TOK, 128), f32),
            vm((2 * TOK, 128), f32),
            vm((2 * TOK, SHARD), f32),
            vm((128, 2 * TOK), bf16),
            vm((N_T, 16, 2 * TOK), bf16),
            vm((TOK, SHARD), bf16),
            vm((TOK, SHARD), bf16),
            vm((HEAD_DIM, TOK), bf16),
            vm((HEAD_DIM, TOK), bf16),
            vm((HEAD_DIM, TOK), bf16),
            vm((HEAD_DIM, TOK), bf16),
            vm((TOK, 128), f32),
            vm((HEADS, TOK, TOK), f32),
            vm((TOK, SHARD), bf16),
            vm((8, TOK, SHARD), bf16),
            vm((8, TOK, SHARD), bf16),
            vm((8, TOK, SHARD), bf16),
            vm((len(SUMS), 144, SHARD), bf16),
            vm((N_T, TOK, SHARD), bf16),
            vm((TOK, SHARD), f32),
            vm((TOK, SHARD), bf16),
            vm((N_T, 16, TOK), bf16),
            vm((N_T, 16, TOK), bf16),
            vm((TOK, 128), bf16),
            vm((N_T, 8, 128), f32),
            vm((N_T, 8, 128), f32),
            vm((8, 128), f32),
            vm((N_DP, 8, 128), f32),
            pltpu.SemaphoreType.DMA((14,)),
        ]
        + [sem] * 22,
        compiler_params=pltpu.CompilerParams(collective_id=1, has_side_effects=True, vmem_limit_bytes=VMEM_BYTES),
    )(*operands)


def finish_body(shard_ref, gn_ref, out_ref, mean_ref):
    out_ref[...] = shard_ref[...]
    mean_ref[...] = gn_ref[...] / (TOK * N_DP)


def finish(shard, gn):
    sds = jax.ShapeDtypeStruct
    return pl.pallas_call(
        finish_body,
        name="finish",
        out_shape=[sds((TOK, SHARD), bf16), sds((4, 128), f32)],
        in_specs=[VM] * 2,
        out_specs=[VM] * 2,
    )(shard, gn)


def tables():
    positions = np.arange(TOK, dtype=np.float32)
    frequency = np.exp(np.float32(-math.log(ROPE_BASE) * 2.0) * np.arange(64, dtype=np.float32) / np.float32(HEAD_DIM))
    angles = positions[:, None] * frequency[None, :].astype(np.float32)
    cosine, sine = np.cos(angles), np.sin(angles)
    return (
        np.concatenate([cosine, cosine], axis=1),
        np.concatenate([-sine, sine], axis=1),
        np.ascontiguousarray(cosine.T),
        np.ascontiguousarray(sine.T),
    )


def on_device(
    hidden_in, norm_gain, clip_base, pct_index, clip_step, w_query, w_key, w_value, w_out, doc_ids
):
    row = lambda v: v.reshape(1, WIDTH)
    tangent_shard, gn = whole(
        hidden_in, row(norm_gain), row(clip_base), row(pct_index), row(clip_step), doc_ids,
        *(jnp.asarray(t) for t in tables()),
        w_query, w_key.T, w_value.T, w_out,
    )
    tangent_shard, gn = finish(tangent_shard, gn)
    return (tangent_shard, gn.reshape(SHARD))


def solution(mesh):
    in_specs = (
        P("dp", "tensor"),
        P(),
        P(),
        P(),
        P(),
        P(None, "tensor"),
        P(None, "tensor"),
        P(None, "tensor"),
        P("tensor", None),
        P("dp", None),
    )
    out_specs = (P("dp", "tensor"), P("tensor"))
    return jax.shard_map(
        on_device, mesh=mesh, in_specs=in_specs, out_specs=out_specs, check_vma=False
    )
```
